128 devices in a mesh: cuts: 4 (over y), idx: 16 (over z_lo, x, core), br: 2 (over z_hi).
Axes of the slice: x: 4, y: 4, z: 4 (z_hi: 2, z_lo: 2; z = z_hi * 2 + z_lo), core: 2. Of those that a mesh axis runs over, the one named last changes fastest.
Arguments:
- stem_mantissa: bfloat16 [4, 2, 1024, 128, 512], P('cuts', None, 'idx', None, 'br'), may hold values from -6 to 6
- exponents: int32 [4, 1024, 128, 4], P('cuts', 'idx', None, 'br'), may hold values from -2 to 2
- branch: bfloat16 [2, 1024, 1024], P(None, None, 'br'), may hold values from -0.125 to 0.125
- closing: bfloat16 [2, 128, 512], P(None, 'idx', 'br'), may hold values from -0.00390625 to 0.00390625
- bitstrings: int32 [1024], replicated, may hold values from 0 to 1023
Outputs:
- new_stem: bfloat16 [4, 2, 1024, 128, 512], P('cuts', None, None, 'idx', 'br')
- amplitudes: float32 [2, 1024], replicated
The draws below stay inside these ranges and needn't reach their ends.
All inputs are finite; a program needn't handle non-finite values.
Results may differ from the reference program's by a relative error of at most 0.0031.
Values may be sent and summed in bfloat16 or wider, within the bound.
A program may use at most 128 MiB of HBM per device.

```python
import jax
import jax.numpy as jnp
from jax import lax

K = 1024
L = 1024
R = 128
Q = 512
NB = 1024
CUTS = 4


def plant(values, rng, smallest, top_value):
    longest = values.shape.index(max(values.shape))
    spots = []
    for shift in (0, 1):
        where = [jax.random.randint(jax.random.fold_in(rng, axis), (), 0, length) for axis, length in enumerate(values.shape)]
        where[longest] = (where[longest] + shift) % values.shape[longest]
        spots.append(tuple(where))
    return values.at[spots[0]].set(smallest).at[spots[1]].set(top_value)


def block_levels(stream_key, shape, cuts, low, largest):
    def one(dim, blocks):
        heights = jax.random.uniform(jax.random.fold_in(jax.random.fold_in(stream_key, 6), dim), (blocks,), jnp.float32, low / len(cuts), largest / len(cuts))
        return jnp.repeat(jnp.exp(heights), shape[dim] // blocks).reshape((-1,) + (1,) * (len(shape) - dim - 1))

    loudness = one(*cuts[0])
    for cut in cuts[1:]:
        loudness = loudness * one(*cut)
    return loudness


def gaussian(key, extent, width, reach, split=(), dtype=jnp.bfloat16):
    array = jax.random.normal(key, extent, jnp.float32) * width
    if len(split) > 0:
        array = block_levels(key, extent, split, -0.22, 0.18) * array
    return jnp.clip(array, min=-reach, max=reach).astype(dtype)


def setup_inputs(seed: int = 0) -> dict:
    seeds = jax.random.split(jax.random.key(seed), 6)
    return {
        "stem_mantissa": gaussian(seeds[0], (CUTS, 2, K, R, Q), 1.0, 6.0, ((0, 4), (2, 16), (4, 2))),
        "exponents": plant(jax.random.randint(seeds[1], (CUTS, K, R, Q // 128), -2, 3), jax.random.fold_in(seeds[1], 1), -2, 2).astype(jnp.int32),
        "branch": gaussian(seeds[2], (2, K, L), (2 * K) ** -0.5, 0.125, ((2, 2),)),
        "closing": gaussian(seeds[3], (2, R, Q), (8 * CUTS * R * Q) ** -0.5, 0.00390625, ((1, 16), (2, 2))),
        "bitstrings": plant(jax.random.randint(seeds[4], (NB,), 0, L), jax.random.fold_in(seeds[4], 1), 0, L - 1).astype(jnp.int32),
    }


def dequantize(mantissa, exponents):
    scale = jnp.exp2(exponents.astype(jnp.float32))
    shaped = mantissa.astype(jnp.float32).reshape(2, K, R, Q // 128, 128) * scale[None, :, :, :, None]
    return shaped.reshape(2, K, R, Q).astype(jnp.bfloat16)


def complex_matrix(block):
    real_part = block[0].T
    imag_part = block[1].T
    upper = jnp.concatenate([real_part, -imag_part], axis=1)
    lower = jnp.concatenate([imag_part, real_part], axis=1)
    return jnp.concatenate([upper, lower], axis=0)


def close_stem(stem_slice, closing):
    fields = stem_slice.astype(jnp.float32)
    env = closing.astype(jnp.float32)
    high = lax.Precision.HIGHEST
    real_part = jnp.einsum('lrq,rq->l', fields[0], env[0], precision=high) - jnp.einsum('lrq,rq->l', fields[1], env[1], precision=high)
    imag_part = jnp.einsum('lrq,rq->l', fields[0], env[1], precision=high) + jnp.einsum('lrq,rq->l', fields[1], env[0], precision=high)
    return jnp.stack([real_part, imag_part])


def reference(stem_mantissa, exponents, branch, closing, bitstrings):
    matrix = complex_matrix(branch)
    total = jnp.zeros((2, L), jnp.float32)
    outputs = []
    for slice_number in range(CUTS):
        values = dequantize(stem_mantissa[slice_number], exponents[slice_number])
        product = jnp.dot(matrix, values.reshape(2 * K, R * Q), preferred_element_type=jnp.float32)
        stem_slice = product.reshape(2, L, R, Q).astype(jnp.bfloat16)
        outputs.append(stem_slice)
        total = total + close_stem(stem_slice, closing)
    amplitudes = total[:, bitstrings]
    return jnp.stack(outputs), amplitudes
```

```python
import jax
import jax.numpy as jnp
from jax import lax
from jax.experimental import pallas as pl
from jax.experimental.pallas import tpu as pltpu
from jax.sharding import PartitionSpec as P

MESH = pl.DeviceIdType.MESH
F32 = jnp.float32
BF16 = jnp.bfloat16
ROUNDS = 8
AHEAD = 3


def full_wait(ref, sem):
    pltpu.make_async_copy(ref, ref, sem).wait()


def contract_kernel(
    stem, expo, branch, closing, bits,
    product, amps,
    inbuf, raw_exp, scale, tiles, sendbuf, recvbuf, own_half, other_half, matrix,
    env_raw, env, bits_v, part, part_in, mid, mid_in, total_in, amps_v,
    in_sem, small_sem, half_sem, send_sem, recv_sem, half_send, half_recv, fwd_send, fwd_recv,
    env_send, env_recv, part_send, part_recv, mid_send, mid_recv, total_send, total_recv, amp_sem,
):
    c = lax.axis_index("cuts")
    me = lax.axis_index("idx")
    b = lax.axis_index("br")
    core = me % 2
    x = (me // 2) % 4
    z = me // 8
    k_local = sendbuf.shape[4]

    def group(n):
        dz = 1 - (n // 2) % 2
        dx = (2 + n % 2) * (1 - n // 4) + (1 - n % 2) * (n // 4)
        return ((z + dz) % 2) * 4 + (x + dx) % 4

    def peer(step):
        return (c, (me + step) % 16, b)

    def outer(step):
        spot = (c * 2 + b + step) % 8
        return (spot // 2, me, spot % 2)

    twin = (c, (me + 8) % 16, 1 - b)
    sibling = (c, me + 1 - 2 * core, b)

    def load(n, slot):
        return pltpu.make_async_copy(
            stem.at[:, :, pl.ds(pl.multiple_of(group(n) * 16, 16), 16), :], inbuf.at[slot], in_sem.at[slot]
        )

    exp_copy = pltpu.make_async_copy(expo, raw_exp, small_sem.at[0])
    exp_copy.start()
    load(0, 0).start()
    load(1, 1).start()

    barrier = pltpu.get_barrier_semaphore()
    for step in range(1, 16):
        pl.semaphore_signal(barrier, inc=1, device_id=peer(step), device_id_type=MESH)
    for step in range(1, 8):
        pl.semaphore_signal(barrier, inc=1, device_id=outer(step), device_id_type=MESH)
    pl.semaphore_signal(barrier, inc=1, device_id=twin, device_id_type=MESH)

    bits_copy = pltpu.make_async_copy(bits, bits_v, small_sem.at[1])
    bits_copy.start()
    own_copy = pltpu.make_async_copy(branch, own_half, half_sem)
    own_copy.start()

    exp_copy.wait()
    for h in range(2):
        shifted = raw_exp[:, h, :] + 2
        low = (1 + shifted % 2).astype(F32)
        middle = (1 + 3 * ((shifted // 2) % 2)).astype(F32)
        high = (1 + 15 * ((shifted // 4) % 2)).astype(F32)
        scale[h] = 0.25 * low * middle * high

    def message(n, dc, j):
        cc = (core + dc) % 2
        return pltpu.make_async_remote_copy(
            src_ref=sendbuf.at[n, cc, j],
            dst_ref=recvbuf.at[j, :, pl.ds(pl.multiple_of(me * k_local, k_local), k_local), :],
            send_sem=send_sem.at[j],
            recv_sem=recv_sem.at[j],
            device_id=(c, group(n) * 2 + cc, b),
            device_id_type=MESH,
        )

    def keep(j):
        return pltpu.make_async_copy(
            sendbuf.at[7, core, j],
            recvbuf.at[j, :, pl.ds(pl.multiple_of(me * k_local, k_local), k_local), :],
            recv_sem.at[j],
        )

    def regroup(n, slot):
        g = group(n)
        turn = (128 - g * 16) % 128
        load(n, slot).wait()

        def step(kb, carry):
            k0 = pl.multiple_of(kb * 16, 16)
            factors = [pltpu.roll(scale[h, pl.ds(k0, 16), :], turn, 1) for h in range(2)]
            for p in range(2):
                for h in range(2):
                    block = inbuf[slot, p, pl.ds(k0, 16), :, h * 128:(h + 1) * 128]
                    tiles[p, h] = block.astype(F32).reshape(256, 128)
            for h in range(2):
                for r in range(16):
                    factor = jnp.broadcast_to(factors[h][:, r:r + 1], (16, 128))
                    for p in range(2):
                        rows = tiles[p, h, pl.ds(r, 16, stride=16), :] * factor
                        sendbuf[n, r // 8, r % 8, p, pl.ds(k0, 16), h * 128:(h + 1) * 128] = rows.astype(BF16)
            return carry

        lax.fori_loop(0, k_local // 16, step, 0)

    regroup(0, 0)
    load(2, 0).start()
    pl.semaphore_wait(barrier, 23)

    def env_copy(step):
        return pltpu.make_async_remote_copy(
            src_ref=closing, dst_ref=env_raw.at[me], send_sem=env_send, recv_sem=env_recv,
            device_id=peer(step), device_id_type=MESH,
        )

    half_rows = own_half.shape[1] // 2
    quarter = half_rows // 4

    def half_copy(t):
        rows = pl.ds(pl.multiple_of(core * half_rows + t * quarter, quarter), quarter)
        return pltpu.make_async_remote_copy(
            src_ref=branch.at[:, rows, :], dst_ref=other_half.at[:, rows, :],
            send_sem=half_send, recv_sem=half_recv, device_id=twin, device_id_type=MESH,
        )

    mine = pl.ds(pl.multiple_of(core * half_rows, half_rows), half_rows)
    theirs = pl.ds(pl.multiple_of((1 - core) * half_rows, half_rows), half_rows)
    forward = pltpu.make_async_remote_copy(
        src_ref=other_half.at[:, mine, :], dst_ref=other_half.at[:, mine, :],
        send_sem=fwd_send, recv_sem=fwd_recv, device_id=sibling, device_id_type=MESH,
    )

    message(0, 0, 0).start()
    message(0, 1, 0).start()
    for t in range(4):
        half_copy(t).start()
    for step in range(1, 16):
        env_copy(step).start()
    pltpu.make_async_copy(closing, env_raw.at[me], env_recv).start()

    def produce(n, carry):
        slot = n % 2
        regroup(n, slot)

        @pl.when(n < 6)
        def _():
            load(n + 2, slot).start()

        message(n, 0, 0).start()
        message(n, 1, 0).start()
        return carry

    lax.fori_loop(1, 7, produce, 0)
    regroup(7, 1)
    keep(0).start()
    message(7, 1, 0).start()

    def send_round(j):
        def one(dc):
            def start(n, carry):
                message(n, dc, j).start()
                return carry

            return start

        lax.fori_loop(0, 7, one(0), 0)
        keep(j).start()
        message(7, 1, j).start()
        lax.fori_loop(0, 7, one(1), 0)

    for j in range(1, AHEAD):
        send_round(j)

    k_all = own_half.shape[1]
    l_half = own_half.shape[2]

    def fill(half, where):
        def step(kb, carry):
            k0 = pl.multiple_of(kb * 128, 128)
            row = pl.multiple_of(where * l_half, l_half)
            real = half[0, pl.ds(k0, 128), :].T
            imag = half[1, pl.ds(k0, 128), :].T
            matrix[pl.ds(row, l_half), pl.ds(k0, 128)] = real
            matrix[pl.ds(row, l_half), pl.ds(k_all + k0, 128)] = -imag
            matrix[pl.ds(2 * l_half + row, l_half), pl.ds(k0, 128)] = imag
            matrix[pl.ds(2 * l_half + row, l_half), pl.ds(k_all + k0, 128)] = real
            return carry

        lax.fori_loop(0, k_all // 128, step, 0)

    own_copy.wait()
    fill(own_half, b)

    full_wait(env_raw, env_recv)
    env[...] = env_raw[...].astype(F32)

    def gather_env(n, sums):
        g = group(n)

        def row(t, sums):
            cc = t // 8
            j = t % 8
            new = []
            for p in range(2):
                values = sendbuf[n, cc, j, p].astype(F32)
                for e in range(2):
                    weighted = values * env[2 * g + cc, e, pl.ds(j, 1), :]
                    new.append(sums[2 * p + e] + (weighted[:, :128] + weighted[:, 128:]))
            return tuple(new)

        return lax.fori_loop(0, 16, row, sums)

    zero = jnp.zeros((k_local, 128), F32)
    sums = lax.fori_loop(0, 8, gather_env, (zero,) * 4)
    w = [jnp.sum(s, axis=1, keepdims=True) for s in sums]
    w_real = w[0] - w[3]
    w_imag = w[1] + w[2]

    full_wait(other_half.at[:, mine, :], half_recv)
    forward.start()
    full_wait(other_half.at[:, theirs, :], fwd_recv)
    fill(other_half, 1 - b)

    k_mine = pl.ds(pl.multiple_of(me * k_local, k_local), k_local)
    blocks = l_half // 128
    for half, where in ((own_half, b), (other_half, 1 - b)):
        real = half[0, k_mine, :].astype(F32)
        imag = half[1, k_mine, :].astype(F32)
        closed_real = jnp.sum(real * w_real - imag * w_imag, axis=0, keepdims=True)
        closed_imag = jnp.sum(real * w_imag + imag * w_real, axis=0, keepdims=True)
        for t in range(blocks):
            part[where * blocks + t] = closed_real[:, t * 128:(t + 1) * 128]
            part[2 * blocks + where * blocks + t] = closed_imag[:, t * 128:(t + 1) * 128]

    def part_copy(step):
        to = (me + step) % 16
        return pltpu.make_async_remote_copy(
            src_ref=part.at[to], dst_ref=part_in.at[me], send_sem=part_send, recv_sem=part_recv,
            device_id=(c, to, b), device_id_type=MESH,
        )

    def mid_copy(step):
        return pltpu.make_async_remote_copy(
            src_ref=mid.at[0], dst_ref=mid_in.at[c * 2 + b], send_sem=mid_send, recv_sem=mid_recv,
            device_id=outer(step), device_id_type=MESH,
        )

    def total_copy(step):
        return pltpu.make_async_remote_copy(
            src_ref=mid.at[1], dst_ref=total_in.at[me], send_sem=total_send, recv_sem=total_recv,
            device_id=peer(step), device_id_type=MESH,
        )

    for step in range(1, 16):
        part_copy(step).start()
    pltpu.make_async_copy(part.at[me], part_in.at[me], part_recv).start()

    def reduce_stage(j):
        @pl.when(j == 2)
        def _():
            full_wait(part_in, part_recv)
            mid[0] = jnp.sum(part_in[...], axis=0)
            for step in range(1, 8):
                mid_copy(step).start()
            pltpu.make_async_copy(mid.at[0], mid_in.at[c * 2 + b], mid_recv).start()

        @pl.when(j == 4)
        def _():
            full_wait(mid_in, mid_recv)
            mid[1] = jnp.sum(mid_in[...], axis=0)
            for step in range(1, 16):
                total_copy(step).start()
            pltpu.make_async_copy(mid.at[1], total_in.at[me], total_recv).start()

        @pl.when(j == 6)
        def _():
            full_wait(total_in, total_recv)
            bits_copy.wait()
            chosen = bits_v[...]
            found = jnp.zeros((8, chosen.shape[1]), F32)
            for t in range(2 * blocks):
                rows = [total_in[t], total_in[2 * blocks + t], jnp.zeros((6, 128), F32)]
                spots = lax.broadcasted_iota(jnp.int32, (128, chosen.shape[1]), 0) + t * 128
                pick = jnp.where(spots == chosen, 1.0, 0.0).astype(F32)
                found = found + jnp.dot(
                    jnp.concatenate(rows, axis=0), pick, precision=lax.Precision.HIGHEST, preferred_element_type=F32
                )
            amps_v[...] = found[:2]
            pltpu.make_async_copy(amps_v, amps, amp_sem).start()

    m_block = 512

    def chunk(j, carry):
        @pl.when(j + AHEAD < ROUNDS)
        def _():
            send_round(j + AHEAD)

        full_wait(recvbuf.at[j], recv_sem.at[j])

        def rows(m, carry):
            m0 = pl.multiple_of(m * m_block, m_block)
            right = recvbuf[j].reshape(2 * k_all, recvbuf.shape[3])
            result = jnp.dot(matrix[pl.ds(m0, m_block), :], right, preferred_element_type=F32)
            for h in range(2):
                product[h, pl.ds(m0 * ROUNDS + j, m_block, stride=ROUNDS), :] = result[:, h * 128:(h + 1) * 128]
            return carry

        lax.fori_loop(0, matrix.shape[0] // m_block, rows, 0)
        reduce_stage(j)
        return carry

    lax.fori_loop(0, ROUNDS, chunk, 0)

    for j in range(ROUNDS):
        full_wait(recvbuf.at[j, :, pl.ds(0, 15 * k_local), :], send_sem.at[j])
    full_wait(other_half.at[:, mine, :], half_send)
    full_wait(other_half.at[:, mine, :], fwd_send)
    full_wait(env_raw.at[pl.ds(0, 15)], env_send)
    full_wait(part_in.at[pl.ds(0, 15)], part_send)
    full_wait(mid_in.at[pl.ds(0, 7)], mid_send)
    full_wait(total_in.at[pl.ds(0, 15)], total_send)
    full_wait(amps_v, amp_sem)


def write_kernel(product, amps_in, out, amps, staging, out_sem):
    blocks, rows = staging.shape[:2]
    per_part = out.shape[1] // rows

    def copy(t):
        return pltpu.make_async_copy(
            staging.at[t], out.at[t // per_part, pl.ds((t % per_part) * rows, rows)], out_sem.at[t]
        )

    def step(t, carry):
        for h in range(2):
            block = product[h, pl.ds(pl.multiple_of(t * rows * 8, rows * 8), rows * 8), :]
            staging[t, :, :, h * 128:(h + 1) * 128] = block.reshape(rows, 8, 128).astype(BF16)
        copy(t).start()
        return carry

    lax.fori_loop(0, blocks, step, 0)
    amps[...] = amps_in[...]

    def finish(t, carry):
        copy(t).wait()
        return carry

    lax.fori_loop(0, blocks, finish, 0)


def shards(stem_mantissa, exponents, branch, closing, bitstrings):
    stem = stem_mantissa[0]
    k_local, r_all, q_local = stem.shape[1:]
    k_all, l_half = branch.shape[1:]
    l_all = 2 * l_half
    r_local = closing.shape[1]
    expo = jnp.transpose(exponents[0], (0, 2, 1))
    bits = bitstrings.reshape(1, -1)
    dma = pltpu.SemaphoreType.DMA
    hbm = pl.BlockSpec(memory_space=pl.ANY)
    vmem = pl.BlockSpec(memory_space=pltpu.VMEM)
    product, amps = pl.pallas_call(
        contract_kernel,
        out_shape=(
            pltpu.VMEM((2, 2 * l_all * r_local, 128), F32),
            jax.ShapeDtypeStruct((2, bits.shape[1]), F32),
        ),
        in_specs=[hbm] * 5,
        out_specs=(vmem, hbm),
        scratch_shapes=[
            pltpu.VMEM((2, 2, k_local, 16, q_local), BF16),
            pltpu.VMEM(expo.shape, jnp.int32),
            pltpu.VMEM((2, k_local, r_all), F32),
            pltpu.VMEM((2, 2, 256, 128), F32),
            pltpu.VMEM((8, 2, r_local, 2, k_local, q_local), BF16),
            pltpu.VMEM((r_local, 2, k_all, q_local), BF16),
            pltpu.VMEM((2, k_all, l_half), BF16),
            pltpu.VMEM((2, k_all, l_half), BF16),
            pltpu.VMEM((2 * l_all, 2 * k_all), BF16),
            pltpu.VMEM((16,) + closing.shape, BF16),
            pltpu.VMEM((16,) + closing.shape, F32),
            pltpu.VMEM(bits.shape, jnp.int32),
            pltpu.VMEM((16, 1, 128), F32),
            pltpu.VMEM((16, 1, 128), F32),
            pltpu.VMEM((2, 1, 128), F32),
            pltpu.VMEM((8, 1, 128), F32),
            pltpu.VMEM((16, 1, 128), F32),
            pltpu.VMEM((2, bits.shape[1]), F32),
            dma((2,)), dma((2,)), dma,
            dma((ROUNDS,)), dma((ROUNDS,)),
            dma, dma, dma, dma, dma, dma, dma, dma, dma, dma, dma, dma, dma,
        ],
        compiler_params=pltpu.CompilerParams(
            collective_id=0, has_side_effects=True, vmem_limit_bytes=44 * 2**20
        ),
        cost_estimate=pl.CostEstimate(
            flops=2 * (2 * k_all) * (2 * l_all) * r_local * q_local, bytes_accessed=2 * stem.size, transcendentals=0
        ),
        name="exchange_and_contract",
    )(stem, expo, branch, closing, bits)

    rows = 128
    new_block, amps = pl.pallas_call(
        write_kernel,
        out_shape=(
            jax.ShapeDtypeStruct((2, l_all, r_local, q_local), BF16),
            jax.ShapeDtypeStruct(amps.shape, F32),
        ),
        in_specs=[vmem, vmem],
        out_specs=(hbm, vmem),
        scratch_shapes=[
            pltpu.VMEM((2 * l_all // rows, rows, r_local, q_local), BF16),
            dma((2 * l_all // rows,)),
        ],
        compiler_params=pltpu.CompilerParams(vmem_limit_bytes=40 * 2**20),
        name="round_and_write",
    )(pltpu.with_memory_space_constraint(product, pltpu.VMEM), amps)
    return (new_block[None], amps)


def solution(mesh):
    return jax.shard_map(
        shards,
        mesh=mesh,
        in_specs=(
            P("cuts", None, "idx", None, "br"),
            P("cuts", "idx", None, "br"),
            P(None, None, "br"),
            P(None, "idx", "br"),
            P(),
        ),
        out_specs=(P("cuts", None, None, "idx", "br"), P()),
        check_vma=False,
    )
```

```python
import jax
import jax.numpy as jnp
from jax import lax
from jax.experimental import pallas as pl
from jax.experimental.pallas import tpu as pltpu
from jax.sharding import PartitionSpec as P

MESH = pl.DeviceIdType.MESH
F32 = jnp.float32
BF16 = jnp.bfloat16
ROUNDS = 8
DEPTH = 2


def full_wait(ref, sem):
    pltpu.make_async_copy(ref, ref, sem).wait()


def contract_kernel(
    stem, expo, branch, closing, bits,
    product, latest, matrix, amps,
    inbuf, raw_exp, scale, tiles, sendbuf, recvbuf, own_half, other_half, other_rows,
    env_raw, env, bits_v, part, part_in, mid, mid_in, total_in, amps_v,
    in_sem, small_sem, half_sem, send_sem, recv_sem, near_send, half_send, half_recv, fwd_send, fwd_recv,
    rows_send, rows_recv, env_send, env_recv, share_send, share_recv, part_send, part_recv, mid_send, mid_recv, total_send, total_recv, amp_sem,
    ready, twin_ready,
):
    c = lax.axis_index("cuts")
    me = lax.axis_index("idx")
    b = lax.axis_index("br")
    core = me % 2
    x = (me // 2) % 4
    z = me // 8
    k_local, q_local = sendbuf.shape[4:]

    def group(n):
        dz = 1 - (n // 2) % 2
        dx = (2 + n % 2) * (1 - n // 4) + (1 - n % 2) * (n // 4)
        return ((z + dz) % 2) * 4 + (x + dx) % 4

    def peer(step):
        return (c, (me + step) % 16, b)

    rank = b * 4 + c

    def outer(q):
        return (q % 4, me, q // 4)

    twin = (c, (me + 8) % 16, 1 - b)
    sibling = (c, me + 1 - 2 * core, b)

    def load(n, slot):
        return pltpu.make_async_copy(
            stem.at[:, :, pl.ds(pl.multiple_of(group(n) * 16, 16), 16), :], inbuf.at[slot], in_sem.at[slot]
        )

    exp_copy = pltpu.make_async_copy(expo, raw_exp, small_sem.at[0])
    exp_copy.start()
    load(0, 0).start()
    load(1, 1).start()

    barrier = pltpu.get_barrier_semaphore()
    for step in range(1, 16):
        pl.semaphore_signal(barrier, inc=1, device_id=peer(step), device_id_type=MESH)

    @pl.when(b == 0)
    def _():
        pl.semaphore_signal(barrier, inc=1, device_id=twin, device_id_type=MESH)

    for q in range(1, 8):
        @pl.when(q > rank)
        def _(q=q):
            pl.semaphore_signal(barrier, inc=1, device_id=outer(q), device_id_type=MESH)

    bits_copy = pltpu.make_async_copy(bits, bits_v, small_sem.at[1])
    bits_copy.start()
    own_copy = pltpu.make_async_copy(branch, own_half, half_sem)
    own_copy.start()

    exp_copy.wait()
    for h in range(2):
        shifted = raw_exp[:, h, :] + 2
        low = (1 + shifted % 2).astype(F32)
        middle = (1 + 3 * ((shifted // 2) % 2)).astype(F32)
        high = (1 + 15 * ((shifted // 4) % 2)).astype(F32)
        scale[h] = 0.25 * low * middle * high

    def landing(dc, j, final):
        rows = pl.ds(pl.multiple_of((me // 2) * k_local, k_local), k_local)
        return latest.at[dc, :, rows, :] if final else recvbuf.at[j, dc, :, rows, :]

    def message(n, dc, j, sem, final=False):
        cc = (core + dc) % 2
        return pltpu.make_async_remote_copy(
            src_ref=sendbuf.at[n, cc, j],
            dst_ref=landing(dc, j, final),
            send_sem=sem,
            recv_sem=recv_sem.at[2 * j + dc],
            device_id=(c, group(n) * 2 + cc, b),
            device_id_type=MESH,
        )

    def keep(j, final=False):
        return pltpu.make_async_copy(sendbuf.at[7, core, j], landing(0, j, final), recv_sem.at[2 * j])

    def regroup(n, slot):
        g = group(n)
        turn = (128 - g * 16) % 128
        load(n, slot).wait()

        def step(kb, carry):
            k0 = pl.multiple_of(kb * 16, 16)
            factors = [pltpu.roll(scale[h, pl.ds(k0, 16), :], turn, 1) for h in range(2)]
            for p in range(2):
                for h in range(2):
                    block = inbuf[slot, p, pl.ds(k0, 16), :, h * 128:(h + 1) * 128]
                    tiles[p, h] = block.astype(F32).reshape(256, 128)
            for h in range(2):
                for r in range(16):
                    factor = jnp.broadcast_to(factors[h][:, r:r + 1], (16, 128))
                    for p in range(2):
                        rows = tiles[p, h, pl.ds(r, 16, stride=16), :] * factor
                        sendbuf[n, r // 8, r % 8, p, pl.ds(k0, 16), h * 128:(h + 1) * 128] = rows.astype(BF16)
            return carry

        lax.fori_loop(0, k_local // 16, step, 0)

    pl.semaphore_wait(barrier, 15 + rank + b)

    chip = me // 2

    def env_copy(step):
        return pltpu.make_async_remote_copy(
            src_ref=closing, dst_ref=env_raw.at[core, chip], send_sem=env_send, recv_sem=env_recv,
            device_id=peer(2 * step), device_id_type=MESH,
        )

    env_share = pltpu.make_async_remote_copy(
        src_ref=env_raw.at[core], dst_ref=env_raw.at[core], send_sem=share_send, recv_sem=share_recv,
        device_id=sibling, device_id_type=MESH,
    )

    half_rows = own_half.shape[1] // 2
    quarter = half_rows // 4

    def half_copy(t):
        rows = pl.ds(pl.multiple_of(core * half_rows + t * quarter, quarter), quarter)
        return pltpu.make_async_remote_copy(
            src_ref=branch.at[:, rows, :], dst_ref=other_half.at[:, rows, :],
            send_sem=half_send, recv_sem=half_recv, device_id=twin, device_id_type=MESH,
        )

    mine = pl.ds(pl.multiple_of(core * half_rows, half_rows), half_rows)
    theirs = pl.ds(pl.multiple_of((1 - core) * half_rows, half_rows), half_rows)
    forward = pltpu.make_async_remote_copy(
        src_ref=other_half.at[:, mine, :], dst_ref=other_half.at[:, mine, :],
        send_sem=fwd_send, recv_sem=fwd_recv, device_id=sibling, device_id_type=MESH,
    )
    twin_rows = pltpu.make_async_remote_copy(
        src_ref=branch.at[:, pl.ds(pl.multiple_of(((me + 8) % 16) * k_local, k_local), k_local), :],
        dst_ref=other_rows, send_sem=rows_send, recv_sem=rows_recv, device_id=twin, device_id_type=MESH,
    )

    for step in range(1, 8):
        env_copy(step).start()
    pltpu.make_async_copy(closing, env_raw.at[core, chip], env_recv).start()

    @pl.when(b == 1)
    def _():
        pl.semaphore_signal(twin_ready, inc=1, device_id=twin, device_id_type=MESH)

    for q in range(7):
        @pl.when(q < rank)
        def _(q=q):
            pl.semaphore_signal(ready, inc=1, device_id=outer(q), device_id_type=MESH)

    def produce(n, carry):
        slot = n % 2
        regroup(n, slot)

        @pl.when(n < 6)
        def _():
            load(n + 2, slot).start()

        message(n, 0, 0, send_sem.at[0]).start()
        message(n, 1, 0, send_sem.at[1]).start()

        @pl.when(n == 4)
        def _():
            @pl.when(b == 0)
            def _():
                pl.semaphore_wait(twin_ready, 1)

            twin_rows.start()
            for t in range(4):
                half_copy(t).start()

        return carry

    lax.fori_loop(0, 7, produce, 0)
    regroup(7, 1)
    keep(0).start()
    message(7, 1, 0, near_send).start()

    def issue(h, final=False):
        j = h // 2
        dc = h % 2

        def start(n, carry):
            message(n, dc, j, send_sem.at[h], final).start()
            return carry

        lax.fori_loop(0, 7, start, 0)

        @pl.when(dc == 0)
        def _():
            keep(j, final).start()

        @pl.when(dc == 1)
        def _():
            message(7, 1, j, near_send, final).start()

    def drained(h):
        full_wait(recvbuf.at[0, 0, :, pl.ds(0, 7 * k_local), :], send_sem.at[h])

    k_all = own_half.shape[1]
    l_half = own_half.shape[2]

    def fill(half, where):
        def step(kb, carry):
            parity = kb // 4
            source = 4 * (kb % 4) + (core + parity) % 2
            row = pl.multiple_of(where * l_half, l_half)
            column = pl.multiple_of(parity * k_all + (kb % 4) * 128, 128)

            def turned(p):
                pieces = [
                    half[p, pl.ds(pl.multiple_of((source + extra) * k_local, k_local), k_local), :]
                    for extra in (0, 2)
                ]
                return jnp.concatenate(pieces, axis=0).T

            real = turned(0)
            imag = turned(1)
            matrix[pl.ds(row, l_half), pl.ds(column, 128)] = real
            matrix[pl.ds(row, l_half), pl.ds(k_all // 2 + column, 128)] = -imag
            matrix[pl.ds(2 * l_half + row, l_half), pl.ds(column, 128)] = imag
            matrix[pl.ds(2 * l_half + row, l_half), pl.ds(k_all // 2 + column, 128)] = real
            return carry

        lax.fori_loop(0, k_all // 128, step, 0)

    issue(2)
    full_wait(env_raw.at[core], env_recv)
    env_share.start()
    own_copy.wait()

    for h in range(4 - DEPTH):
        drained(h)
    issue(3)
    full_wait(env_raw.at[1 - core], share_recv)
    env[...] = env_raw[...].astype(F32)

    def gather_env(n, sums):
        g = group(n)

        def row(t, sums):
            cc = t // 8
            j = t % 8
            new = []
            for p in range(2):
                values = sendbuf[n, cc, j, p].astype(F32)
                for e in range(2):
                    weighted = values * env[cc, g, e, pl.ds(j, 1), :]
                    new.append(sums[2 * p + e] + (weighted[:, :128] + weighted[:, 128:]))
            return tuple(new)

        return lax.fori_loop(0, 16, row, sums)

    zero = jnp.zeros((k_local, 128), F32)
    sums = lax.fori_loop(0, 8, gather_env, (zero,) * 4)
    w = [jnp.sum(s, axis=1, keepdims=True) for s in sums]
    w_real = w[0] - w[3]
    w_imag = w[1] + w[2]

    k_mine = pl.ds(pl.multiple_of(me * k_local, k_local), k_local)
    blocks = l_half // 128
    full_wait(other_rows, rows_recv)
    for half, rows, where in ((own_half, k_mine, b), (other_rows, slice(None), 1 - b)):
        real = half[0, rows, :].astype(F32)
        imag = half[1, rows, :].astype(F32)
        closed_real = jnp.sum(real * w_real - imag * w_imag, axis=0, keepdims=True)
        closed_imag = jnp.sum(real * w_imag + imag * w_real, axis=0, keepdims=True)
        for t in range(blocks):
            part[where * blocks + t] = closed_real[:, t * 128:(t + 1) * 128]
            part[2 * blocks + where * blocks + t] = closed_imag[:, t * 128:(t + 1) * 128]

    def part_copy(step):
        to = (me + step) % 16
        return pltpu.make_async_remote_copy(
            src_ref=part.at[to], dst_ref=part_in.at[me], send_sem=part_send, recv_sem=part_recv,
            device_id=(c, to, b), device_id_type=MESH,
        )

    def mid_copy(q):
        return pltpu.make_async_remote_copy(
            src_ref=mid.at[0], dst_ref=mid_in.at[rank], send_sem=mid_send, recv_sem=mid_recv,
            device_id=outer(q), device_id_type=MESH,
        )

    def total_copy(step):
        return pltpu.make_async_remote_copy(
            src_ref=mid.at[1], dst_ref=total_in.at[me], send_sem=total_send, recv_sem=total_recv,
            device_id=peer(step), device_id_type=MESH,
        )

    for step in range(1, 16):
        part_copy(step).start()
    pltpu.make_async_copy(part.at[me], part_in.at[me], part_recv).start()

    drained(4 - DEPTH)
    issue(4)
    fill(own_half, b)

    drained(5 - DEPTH)
    issue(5)
    full_wait(part_in, part_recv)
    mid[0] = jnp.sum(part_in[...], axis=0)

    @pl.when(rank < 7)
    def _():
        pl.semaphore_wait(ready, 7 - rank)

    for q in range(8):
        @pl.when(q != rank)
        def _(q=q):
            mid_copy(q).start()

    pltpu.make_async_copy(mid.at[0], mid_in.at[rank], mid_recv).start()

    drained(6 - DEPTH)
    issue(6)
    full_wait(other_half.at[:, mine, :], half_recv)
    forward.start()
    full_wait(mid_in, mid_recv)
    mid[1] = jnp.sum(mid_in[...], axis=0)
    for step in range(1, 16):
        total_copy(step).start()
    pltpu.make_async_copy(mid.at[1], total_in.at[me], total_recv).start()

    drained(7 - DEPTH)
    issue(7)
    full_wait(other_half.at[:, theirs, :], fwd_recv)
    fill(other_half, 1 - b)

    drained(8 - DEPTH)
    issue(8)

    def choose():
        full_wait(total_in, total_recv)
        bits_copy.wait()
        chosen = bits_v[...]
        found = jnp.zeros((8, chosen.shape[1]), F32)
        for t in range(2 * blocks):
            rows = [total_in[t], total_in[2 * blocks + t], jnp.zeros((6, 128), F32)]
            spots = lax.broadcasted_iota(jnp.int32, (128, chosen.shape[1]), 0) + t * 128
            pick = jnp.where(spots == chosen, 1.0, 0.0).astype(F32)
            found = found + jnp.dot(
                jnp.concatenate(rows, axis=0), pick, precision=lax.Precision.HIGHEST, preferred_element_type=F32
            )
        amps_v[...] = found[:2]
        pltpu.make_async_copy(amps_v, amps, amp_sem).start()

    m_block = 512

    def chunk(j, carry):
        drained(j + 9 - DEPTH)

        @pl.when(j + 9 < 2 * ROUNDS - 2)
        def _():
            issue(j + 9)

        @pl.when(j + 9 >= 2 * ROUNDS - 2)
        def _():
            issue(j + 9, True)

        full_wait(recvbuf.at[j, 0], recv_sem.at[2 * j])
        full_wait(recvbuf.at[j, 1], recv_sem.at[2 * j + 1])

        def rows(m, carry):
            m0 = pl.multiple_of(m * m_block, m_block)
            right = recvbuf[j].reshape(2 * k_all, q_local)
            result = jnp.dot(matrix[pl.ds(m0, m_block), :], right, preferred_element_type=F32)
            for h in range(2):
                product[h, pl.ds(m0 * ROUNDS + j, m_block, stride=ROUNDS), :] = result[:, h * 128:(h + 1) * 128]
            return carry

        lax.fori_loop(0, matrix.shape[0] // m_block, rows, 0)

        @pl.when(j == 2)
        def _():
            choose()

        return carry

    lax.fori_loop(0, ROUNDS - 1, chunk, 0)

    def early_rows(m, carry):
        m0 = pl.multiple_of(m * m_block, m_block)
        right = latest[0].reshape(k_all, q_local)
        result = jnp.dot(matrix[pl.ds(m0, m_block), :k_all], right, preferred_element_type=F32)
        for h in range(2):
            spots = pl.ds(m0 * ROUNDS + ROUNDS - 1, m_block, stride=ROUNDS)
            product[h, spots, :] = result[:, h * 128:(h + 1) * 128]
        return carry

    full_wait(latest.at[0], recv_sem.at[2 * ROUNDS - 2])
    lax.fori_loop(0, matrix.shape[0] // m_block, early_rows, 0)
    full_wait(latest.at[1], recv_sem.at[2 * ROUNDS - 1])

    for h in range(2 * ROUNDS - DEPTH, 2 * ROUNDS):
        drained(h)
    full_wait(sendbuf.at[7, 0], near_send)
    full_wait(other_rows, rows_send)
    full_wait(env_raw.at[core], share_send)
    full_wait(other_half.at[:, mine, :], half_send)
    full_wait(other_half.at[:, mine, :], fwd_send)
    full_wait(env_raw.at[0, pl.ds(0, 7)], env_send)
    full_wait(part_in.at[pl.ds(0, 15)], part_send)
    full_wait(mid_in.at[pl.ds(0, 7)], mid_send)
    full_wait(total_in.at[pl.ds(0, 15)], total_send)
    full_wait(amps_v, amp_sem)


def write_kernel(product, latest, matrix, amps_in, out, amps, staging, spread, out_sem, amp_sem):
    amp_copy = pltpu.make_async_copy(amps_in, amps, amp_sem)
    amp_copy.start()
    blocks, rows = staging.shape[:2]
    per_part = out.shape[1] // rows
    half = matrix.shape[1] // 2
    last = ROUNDS - 1
    copies = []
    for t in range(blocks):
        right = latest[1].reshape(half, latest.shape[3])
        result = jnp.dot(matrix[t * rows:(t + 1) * rows, half:], right, preferred_element_type=F32)
        slot = t % 2
        for h in range(2):
            spread[slot, h, pl.ds(last, rows, stride=ROUNDS), :] = result[:, h * 128:(h + 1) * 128]
        for h in range(2):
            before = product[h, t * rows * ROUNDS:(t + 1) * rows * ROUNDS, :].reshape(rows, ROUNDS, 128)
            newest = spread[slot, h].reshape(rows, ROUNDS, 128)
            spot = lax.broadcasted_iota(jnp.int32, (rows, ROUNDS, 128), 1)
            whole = before + jnp.where(spot == last, newest, 0.0)
            staging[t, :, :, h * 128:(h + 1) * 128] = whole.astype(BF16)
        copy = pltpu.make_async_copy(
            staging.at[t], out.at[t // per_part, (t % per_part) * rows:(t % per_part + 1) * rows], out_sem.at[t]
        )
        copy.start()
        copies.append(copy)
    for copy in copies:
        copy.wait()
    amp_copy.wait()


def shards(stem_mantissa, exponents, branch, closing, bitstrings):
    stem = stem_mantissa[0]
    k_local, r_all, q_local = stem.shape[1:]
    k_all, l_half = branch.shape[1:]
    l_all = 2 * l_half
    r_local = closing.shape[1]
    expo = jnp.transpose(exponents[0], (0, 2, 1))
    bits = bitstrings.reshape(1, -1)
    dma = pltpu.SemaphoreType.DMA
    hbm = pl.BlockSpec(memory_space=pl.ANY)
    vmem = pl.BlockSpec(memory_space=pltpu.VMEM)
    product, received, matrix, amps = pl.pallas_call(
        contract_kernel,
        out_shape=(
            pltpu.VMEM((2, 2 * l_all * r_local, 128), F32),
            pltpu.VMEM((2, 2, k_all // 2, q_local), BF16),
            pltpu.VMEM((2 * l_all, 2 * k_all), BF16),
            jax.ShapeDtypeStruct((2, bits.shape[1]), F32),
        ),
        in_specs=[hbm] * 5,
        out_specs=(vmem, vmem, vmem, hbm),
        scratch_shapes=[
            pltpu.VMEM((2, 2, k_local, 16, q_local), BF16),
            pltpu.VMEM(expo.shape, jnp.int32),
            pltpu.VMEM((2, k_local, r_all), F32),
            pltpu.VMEM((2, 2, 256, 128), F32),
            pltpu.VMEM((8, 2, r_local, 2, k_local, q_local), BF16),
            pltpu.VMEM((r_local - 1, 2, 2, k_all // 2, q_local), BF16),
            pltpu.VMEM((2, k_all, l_half), BF16),
            pltpu.VMEM((2, k_all, l_half), BF16),
            pltpu.VMEM((2, k_local, l_half), BF16),
            pltpu.VMEM((2, 8) + closing.shape, BF16),
            pltpu.VMEM((2, 8) + closing.shape, F32),
            pltpu.VMEM(bits.shape, jnp.int32),
            pltpu.VMEM((16, 1, 128), F32),
            pltpu.VMEM((16, 1, 128), F32),
            pltpu.VMEM((2, 1, 128), F32),
            pltpu.VMEM((8, 1, 128), F32),
            pltpu.VMEM((16, 1, 128), F32),
            pltpu.VMEM((2, bits.shape[1]), F32),
            dma((2,)), dma((2,)), dma,
            dma((2 * ROUNDS,)), dma((2 * ROUNDS,)),
            dma, dma, dma, dma, dma, dma, dma, dma, dma, dma, dma, dma, dma, dma, dma, dma, dma, dma,
            pltpu.SemaphoreType.REGULAR, pltpu.SemaphoreType.REGULAR,
        ],
        compiler_params=pltpu.CompilerParams(
            collective_id=0, has_side_effects=True, vmem_limit_bytes=30 * 2**20
        ),
        cost_estimate=pl.CostEstimate(
            flops=2 * (2 * k_all) * (2 * l_all) * r_local * q_local, bytes_accessed=2 * stem.size, transcendentals=0
        ),
        name="exchange_and_contract",
    )(stem, expo, branch, closing, bits)

    rows = 256
    keep_vmem = [pltpu.with_memory_space_constraint(a, pltpu.VMEM) for a in (product, received, matrix)]
    new_block, amps = pl.pallas_call(
        write_kernel,
        out_shape=(
            jax.ShapeDtypeStruct((2, l_all, r_local, q_local), BF16),
            jax.ShapeDtypeStruct(amps.shape, F32),
        ),
        in_specs=[vmem, vmem, vmem, hbm],
        out_specs=(hbm, hbm),
        scratch_shapes=[
            pltpu.VMEM((2 * l_all // rows, rows, r_local, q_local), BF16),
            pltpu.VMEM((2, 2, rows * r_local, 128), F32),
            dma((2 * l_all // rows,)),
            dma,
        ],
        compiler_params=pltpu.CompilerParams(vmem_limit_bytes=30 * 2**20),
        name="finish_and_write",
    )(*keep_vmem, amps)
    return (new_block[None], amps)


def solution(mesh):
    return jax.shard_map(
        shards,
        mesh=mesh,
        in_specs=(
            P("cuts", None, "idx", None, "br"),
            P("cuts", "idx", None, "br"),
            P(None, None, "br"),
            P(None, "idx", "br"),
            P(),
        ),
        out_specs=(P("cuts", None, None, "idx", "br"), P()),
        check_vma=False,
    )
```

```python
import jax
import jax.numpy as jnp
from jax import lax
from jax.experimental import pallas as pl
from jax.experimental.pallas import tpu as pltpu
from jax.sharding import PartitionSpec as P

MESH = pl.DeviceIdType.MESH
F32 = jnp.float32
BF16 = jnp.bfloat16
ROUNDS = 8
DEPTH = 2
SLOTS = 4


def full_wait(ref, sem):
    pltpu.make_async_copy(ref, ref, sem).wait()


def contract_kernel(
    stem, expo, branch, closing, bits,
    done, product, latest, matrix, amps,
    inbuf, raw_exp, scale, tiles, sendbuf, recvbuf, first, own_half, other_half, other_rows,
    env_raw, env, bits_v, part, part_in, mid, mid_in, total_in, amps_v,
    in_sem, small_sem, half_sem, send_sem, recv_sem, near_send, half_send, half_recv, fwd_send, fwd_recv,
    rows_send, rows_recv, env_send, env_recv, share_send, share_recv, part_send, part_recv, mid_send, mid_recv, total_send, total_recv, amp_sem,
    ready, twin_ready,
):
    c = lax.axis_index("cuts")
    me = lax.axis_index("idx")
    b = lax.axis_index("br")
    core = me % 2
    x = (me // 2) % 4
    z = me // 8
    k_local, q_local = sendbuf.shape[4:]

    def group(n):
        dz = 1 - (n // 2) % 2
        dx = (2 + n % 2) * (1 - n // 4) + (1 - n % 2) * (n // 4)
        return ((z + dz) % 2) * 4 + (x + dx) % 4

    def source_group(n):
        dz = 1 - (n // 2) % 2
        dx = (2 + n % 2) * (1 - n // 4) + (1 - n % 2) * (n // 4)
        return ((z + dz) % 2) * 4 + (x + 4 - dx) % 4

    def peer(step):
        return (c, (me + step) % 16, b)

    rank = b * 4 + c

    def outer(q):
        return (q % 4, me, q // 4)

    twin = (c, (me + 8) % 16, 1 - b)
    sibling = (c, me + 1 - 2 * core, b)

    def load(step):
        rows = pl.ds(pl.multiple_of(group(step % 8) * 16, 16), 16)
        columns = pl.ds(pl.multiple_of((step // 8) * 128, 128), 128)
        slot = step % SLOTS
        return pltpu.make_async_copy(stem.at[:, :, rows, columns], inbuf.at[slot], in_sem.at[slot])

    exp_copy = pltpu.make_async_copy(expo, raw_exp, small_sem.at[0])
    exp_copy.start()
    for step in range(SLOTS):
        load(step).start()

    barrier = pltpu.get_barrier_semaphore()
    for step in range(1, 16):
        pl.semaphore_signal(barrier, inc=1, device_id=peer(step), device_id_type=MESH)

    @pl.when(b == 0)
    def _():
        pl.semaphore_signal(barrier, inc=1, device_id=twin, device_id_type=MESH)

    for q in range(1, 8):
        @pl.when(q > rank)
        def _(q=q):
            pl.semaphore_signal(barrier, inc=1, device_id=outer(q), device_id_type=MESH)

    bits_copy = pltpu.make_async_copy(bits, bits_v, small_sem.at[1])
    bits_copy.start()
    own_copy = pltpu.make_async_copy(branch, own_half, half_sem)
    own_copy.start()

    exp_copy.wait()
    for h in range(2):
        shifted = raw_exp[:, h, :] + 2
        low = (1 + shifted % 2).astype(F32)
        middle = (1 + 3 * ((shifted // 2) % 2)).astype(F32)
        high = (1 + 15 * ((shifted // 4) % 2)).astype(F32)
        scale[h] = 0.25 * low * middle * high

    def landing(n, dc, j, final):
        rows = pl.ds(pl.multiple_of((n % 4) * k_local, k_local), k_local)
        quarter = 2 * dc + n // 4
        return latest.at[quarter, :, rows, :] if final else recvbuf.at[j, quarter, :, rows, :]

    def message(n, dc, j, sem, final=False):
        cc = (core + dc) % 2
        return pltpu.make_async_remote_copy(
            src_ref=sendbuf.at[n, cc, j],
            dst_ref=landing(n, dc, j, final),
            send_sem=sem,
            recv_sem=recv_sem.at[4 * j + 2 * dc + n // 4],
            device_id=(c, group(n) * 2 + cc, b),
            device_id_type=MESH,
        )

    def keep(j, final=False):
        return pltpu.make_async_copy(sendbuf.at[7, core, j], landing(7, 0, j, final), recv_sem.at[4 * j + 1])

    def regroup(step):
        n = step % 8
        h = step // 8
        slot = step % SLOTS
        turn = (128 - group(n) * 16) % 128
        load(step).wait()

        def part_of_k(kb, carry):
            k0 = pl.multiple_of(kb * 16, 16)
            factors = pltpu.roll(scale[h, pl.ds(k0, 16), :], turn, 1)
            for p in range(2):
                tiles[p] = inbuf[slot, p, pl.ds(k0, 16)].astype(F32).reshape(256, 128)
            for r in range(16):
                factor = jnp.broadcast_to(factors[:, r:r + 1], (16, 128))
                spot = (r % 2) * 128
                for p in range(2):
                    rows = tiles[p, pl.ds(r, 16, stride=16), :] * factor
                    sendbuf[n, r // 8, 4 * h + r % 8 // 2, p, pl.ds(k0, 16), spot:spot + 128] = rows.astype(BF16)
            return carry

        lax.fori_loop(0, k_local // 16, part_of_k, 0)

    regroup(0)
    load(SLOTS).start()
    pl.semaphore_wait(barrier, 15 + rank + b)

    chip = me // 2

    def env_copy(step):
        return pltpu.make_async_remote_copy(
            src_ref=closing, dst_ref=env_raw.at[core, chip], send_sem=env_send, recv_sem=env_recv,
            device_id=peer(2 * step), device_id_type=MESH,
        )

    env_share = pltpu.make_async_remote_copy(
        src_ref=env_raw.at[core], dst_ref=env_raw.at[core], send_sem=share_send, recv_sem=share_recv,
        device_id=sibling, device_id_type=MESH,
    )

    half_rows = own_half.shape[1] // 2
    quarter = half_rows // 4

    def half_copy(t):
        rows = pl.ds(pl.multiple_of(core * half_rows + t * quarter, quarter), quarter)
        return pltpu.make_async_remote_copy(
            src_ref=branch.at[:, rows, :], dst_ref=other_half.at[:, rows, :],
            send_sem=half_send, recv_sem=half_recv, device_id=twin, device_id_type=MESH,
        )

    mine = pl.ds(pl.multiple_of(core * half_rows, half_rows), half_rows)
    theirs = pl.ds(pl.multiple_of((1 - core) * half_rows, half_rows), half_rows)
    forward = pltpu.make_async_remote_copy(
        src_ref=other_half.at[:, mine, :], dst_ref=other_half.at[:, mine, :],
        send_sem=fwd_send, recv_sem=fwd_recv, device_id=sibling, device_id_type=MESH,
    )
    twin_rows = pltpu.make_async_remote_copy(
        src_ref=branch.at[:, pl.ds(pl.multiple_of(((me + 8) % 16) * k_local, k_local), k_local), :],
        dst_ref=other_rows, send_sem=rows_send, recv_sem=rows_recv, device_id=twin, device_id_type=MESH,
    )


    @pl.when(b == 1)
    def _():
        pl.semaphore_signal(twin_ready, inc=1, device_id=twin, device_id_type=MESH)

    for q in range(7):
        @pl.when(q < rank)
        def _(q=q):
            pl.semaphore_signal(ready, inc=1, device_id=outer(q), device_id_type=MESH)

    message(0, 0, 0, send_sem.at[0]).start()
    message(0, 1, 0, send_sem.at[1]).start()
    for step in range(1, 8):
        env_copy(step).start()
    pltpu.make_async_copy(closing, env_raw.at[core, chip], env_recv).start()

    def produce(n, carry):
        regroup(n)
        load(n + SLOTS).start()
        message(n, 0, 0, send_sem.at[0]).start()
        message(n, 1, 0, send_sem.at[1]).start()

        @pl.when(n == 4)
        def _():
            @pl.when(b == 0)
            def _():
                pl.semaphore_wait(twin_ready, 1)

            twin_rows.start()
            for t in range(4):
                half_copy(t).start()

        return carry

    lax.fori_loop(1, 7, produce, 0)
    regroup(7)
    load(7 + SLOTS).start()
    keep(0).start()
    message(7, 1, 0, near_send).start()

    def issue(h, final=False):
        j = h // 2
        dc = h % 2

        def start(n, carry):
            message(n, dc, j, send_sem.at[h], final).start()
            return carry

        lax.fori_loop(0, 7, start, 0)

        @pl.when(dc == 0)
        def _():
            keep(j, final).start()

        @pl.when(dc == 1)
        def _():
            message(7, 1, j, near_send, final).start()

    def drained(h):
        full_wait(sendbuf.at[0, 0, pl.ds(0, 7)], send_sem.at[h])

    k_all = own_half.shape[1]
    l_half = own_half.shape[2]

    def fill(half, where):
        def step(kb, carry):
            quarter = kb // 2
            place = (quarter % 2) * 4 + (kb % 2) * 2
            row = pl.multiple_of(where * l_half, l_half)
            column = pl.multiple_of(quarter * (k_all // 2) + (kb % 2) * 128, 128)

            def turned(p):
                pieces = []
                for extra in (0, 1):
                    source = 2 * source_group(place + extra) + (core + quarter // 2) % 2
                    pieces.append(half[p, pl.ds(pl.multiple_of(source * k_local, k_local), k_local), :])
                return jnp.concatenate(pieces, axis=0).T

            real = turned(0)
            imag = turned(1)
            matrix[pl.ds(row, l_half), pl.ds(column, 128)] = real
            matrix[pl.ds(row, l_half), pl.ds(k_all // 4 + column, 128)] = -imag
            matrix[pl.ds(2 * l_half + row, l_half), pl.ds(column, 128)] = imag
            matrix[pl.ds(2 * l_half + row, l_half), pl.ds(k_all // 4 + column, 128)] = real
            return carry

        lax.fori_loop(0, k_all // 128, step, 0)

    issue(2)

    def second_half(step, carry):
        regroup(step)

        @pl.when(step + SLOTS < 16)
        def _():
            load(step + SLOTS).start()

        return carry

    lax.fori_loop(8, 16, second_half, 0)
    full_wait(env_raw.at[core], env_recv)
    env_share.start()
    own_copy.wait()

    for h in range(4 - DEPTH):
        drained(h)
    issue(3)
    full_wait(env_raw.at[1 - core], share_recv)
    for h in range(2):
        env[:, :, :, h] = env_raw[:, :, :, :, h * 128:(h + 1) * 128].astype(F32)

    def gather_env(n, sums):
        g = group(n)

        def row(t, sums):
            cc = t // 4
            pair = t % 4
            new = list(sums)
            for h in range(2):
                for p in range(2):
                    values = sendbuf[n, cc, 4 * h + pair, p].astype(F32)
                    for e in range(2):
                        for s in range(2):
                            weight = env[cc, g, e, h, pl.ds(2 * pair + s, 1), :]
                            new[2 * p + e] = new[2 * p + e] + values[:, s * 128:(s + 1) * 128] * weight
            return tuple(new)

        return lax.fori_loop(0, 8, row, sums)

    zero = jnp.zeros((k_local, 128), F32)
    sums = lax.fori_loop(0, 8, gather_env, (zero,) * 4)
    w = [jnp.sum(s, axis=1, keepdims=True) for s in sums]
    w_real = w[0] - w[3]
    w_imag = w[1] + w[2]

    k_mine = pl.ds(pl.multiple_of(me * k_local, k_local), k_local)
    blocks = l_half // 128
    full_wait(other_rows, rows_recv)
    for half, rows, where in ((own_half, k_mine, b), (other_rows, slice(None), 1 - b)):
        real = half[0, rows, :].astype(F32)
        imag = half[1, rows, :].astype(F32)
        closed_real = jnp.sum(real * w_real - imag * w_imag, axis=0, keepdims=True)
        closed_imag = jnp.sum(real * w_imag + imag * w_real, axis=0, keepdims=True)
        for t in range(blocks):
            part[where * blocks + t] = closed_real[:, t * 128:(t + 1) * 128]
            part[2 * blocks + where * blocks + t] = closed_imag[:, t * 128:(t + 1) * 128]

    def part_copy(step):
        to = (me + step) % 16
        return pltpu.make_async_remote_copy(
            src_ref=part.at[to], dst_ref=part_in.at[me], send_sem=part_send, recv_sem=part_recv,
            device_id=(c, to, b), device_id_type=MESH,
        )

    def mid_copy(q):
        return pltpu.make_async_remote_copy(
            src_ref=mid.at[0], dst_ref=mid_in.at[rank], send_sem=mid_send, recv_sem=mid_recv,
            device_id=outer(q), device_id_type=MESH,
        )

    def total_copy(step):
        return pltpu.make_async_remote_copy(
            src_ref=mid.at[1], dst_ref=total_in.at[me], send_sem=total_send, recv_sem=total_recv,
            device_id=peer(step), device_id_type=MESH,
        )

    for step in range(1, 16):
        part_copy(step).start()
    pltpu.make_async_copy(part.at[me], part_in.at[me], part_recv).start()

    drained(4 - DEPTH)
    issue(4)
    fill(own_half, b)

    drained(5 - DEPTH)
    issue(5)
    full_wait(part_in, part_recv)
    mid[0] = jnp.sum(part_in[...], axis=0)

    @pl.when(rank < 7)
    def _():
        pl.semaphore_wait(ready, 7 - rank)

    for q in range(8):
        @pl.when(q != rank)
        def _(q=q):
            mid_copy(q).start()

    pltpu.make_async_copy(mid.at[0], mid_in.at[rank], mid_recv).start()

    drained(6 - DEPTH)
    issue(6)
    full_wait(other_half.at[:, mine, :], half_recv)
    forward.start()
    full_wait(mid_in, mid_recv)
    mid[1] = jnp.sum(mid_in[...], axis=0)
    for step in range(1, 16):
        total_copy(step).start()
    pltpu.make_async_copy(mid.at[1], total_in.at[me], total_recv).start()

    drained(7 - DEPTH)
    issue(7)
    full_wait(other_half.at[:, theirs, :], fwd_recv)
    fill(other_half, 1 - b)

    drained(8 - DEPTH)
    issue(8)

    def choose():
        full_wait(total_in, total_recv)
        bits_copy.wait()
        chosen = bits_v[...]
        found = jnp.zeros((8, chosen.shape[1]), F32)
        for t in range(2 * blocks):
            rows = [total_in[t], total_in[2 * blocks + t], jnp.zeros((6, 128), F32)]
            spots = lax.broadcasted_iota(jnp.int32, (128, chosen.shape[1]), 0) + t * 128
            pick = jnp.where(spots == chosen, 1.0, 0.0).astype(F32)
            found = found + jnp.dot(
                jnp.concatenate(rows, axis=0), pick, precision=lax.Precision.HIGHEST, preferred_element_type=F32
            )
        amps_v[...] = found[:2]
        pltpu.make_async_copy(amps_v, amps, amp_sem).start()

    m_block = 512

    def tile_rows(m0, j, s):
        return pl.ds(m0 * ROUNDS + 2 * (j % 4) + s, m_block, stride=ROUNDS)

    def chunk(target):
        def run(j, carry):
            drained(j + 9 - DEPTH)

            @pl.when(j + 9 < 2 * ROUNDS - 2)
            def _():
                issue(j + 9)

            @pl.when(j + 9 >= 2 * ROUNDS - 2)
            def _():
                issue(j + 9, True)

            for quarter in range(4):
                full_wait(recvbuf.at[j, quarter], recv_sem.at[4 * j + quarter])

            def rows(m, carry):
                m0 = pl.multiple_of(m * m_block, m_block)
                right = recvbuf[j].reshape(2 * k_all, q_local)
                result = jnp.dot(matrix[pl.ds(m0, m_block), :], right, preferred_element_type=F32)
                for s in range(2):
                    target[tile_rows(m0, j, s), :] = result[:, s * 128:(s + 1) * 128]
                return carry

            lax.fori_loop(0, matrix.shape[0] // m_block, rows, 0)

            @pl.when(j == 2)
            def _():
                choose()

            return carry

        return run

    lax.fori_loop(0, ROUNDS // 2, chunk(first), 0)

    def settle(t, carry):
        t0 = pl.multiple_of(t * 128, 128)
        block = first[pl.ds(pl.multiple_of(t0 * ROUNDS, 128 * ROUNDS), 128 * ROUNDS), :]
        done[pl.ds(t0, 128)] = block.reshape(128, ROUNDS, 128).astype(BF16)
        return carry

    lax.fori_loop(0, matrix.shape[0] // 128, settle, 0)
    lax.fori_loop(ROUNDS // 2, ROUNDS - 1, chunk(product), 0)

    def early(low, high):
        columns = slice(low * (k_all // 2), high * (k_all // 2))

        def rows(m, carry):
            m0 = pl.multiple_of(m * m_block, m_block)
            right = latest[low:high].reshape((high - low) * (k_all // 2), q_local)
            result = jnp.dot(matrix[pl.ds(m0, m_block), columns], right, preferred_element_type=F32)
            for s in range(2):
                spots = tile_rows(m0, ROUNDS - 1, s)
                piece = result[:, s * 128:(s + 1) * 128]
                product[spots, :] = piece if low == 0 else product[spots, :] + piece
            return carry

        lax.fori_loop(0, matrix.shape[0] // m_block, rows, 0)

    last = 4 * (ROUNDS - 1)
    full_wait(latest.at[0], recv_sem.at[last])
    full_wait(latest.at[1], recv_sem.at[last + 1])
    early(0, 2)
    full_wait(latest.at[2], recv_sem.at[last + 2])
    full_wait(latest.at[3], recv_sem.at[last + 3])

    for h in range(2 * ROUNDS - DEPTH, 2 * ROUNDS):
        drained(h)
    full_wait(sendbuf.at[7, 0], near_send)
    full_wait(other_rows, rows_send)
    full_wait(env_raw.at[core], share_send)
    full_wait(other_half.at[:, mine, :], half_send)
    full_wait(other_half.at[:, mine, :], fwd_send)
    full_wait(env_raw.at[0, pl.ds(0, 7)], env_send)
    full_wait(part_in.at[pl.ds(0, 15)], part_send)
    full_wait(mid_in.at[pl.ds(0, 7)], mid_send)
    full_wait(total_in.at[pl.ds(0, 15)], total_send)
    full_wait(amps_v, amp_sem)


def write_kernel(
    done, product, latest, matrix, amps_in, out, amps, staging, spread, done_sem, out_sem, amp_sem
):
    amp_copy = pltpu.make_async_copy(amps_in, amps, amp_sem)
    amp_copy.start()
    blocks, rows = staging.shape[:2]
    l_all = out.shape[1]
    per_part = l_all // rows
    quarter = matrix.shape[1] // 4
    big = spread.shape[0] // ROUNDS
    whole = [
        pltpu.make_async_copy(done.at[pl.ds(p * l_all, l_all)], out.at[p, :, :, pl.ds(0, 128)], done_sem.at[p])
        for p in range(2)
    ]
    for copy in whole:
        copy.start()

    def copy(t):
        return pltpu.make_async_copy(
            staging.at[t],
            out.at[t // per_part, pl.ds((t % per_part) * rows, rows), :, pl.ds(128, 128)],
            out_sem.at[t],
        )

    def block(m, carry):
        m0 = pl.multiple_of(m * big, big)
        right = latest[2:].reshape(2 * quarter, latest.shape[3])
        result = jnp.dot(matrix[pl.ds(m0, big), 2 * quarter:], right, preferred_element_type=F32)
        for s in range(2):
            spread[pl.ds(ROUNDS - 2 + s, big, stride=ROUNDS), :] = result[:, s * 128:(s + 1) * 128]

        def piece(i, carry):
            t = m * (big // rows) + i
            spots = pl.ds(pl.multiple_of(t * rows * ROUNDS, rows * ROUNDS), rows * ROUNDS)
            local = pl.ds(pl.multiple_of(i * rows * ROUNDS, rows * ROUNDS), rows * ROUNDS)
            before = product[spots, :].reshape(rows, ROUNDS, 128)
            newest = spread[local, :].reshape(rows, ROUNDS, 128)
            spot = lax.broadcasted_iota(jnp.int32, (rows, ROUNDS, 128), 1)
            staging[t] = (before + jnp.where(spot >= ROUNDS - 2, newest, 0.0)).astype(BF16)
            copy(t).start()
            return carry

        lax.fori_loop(0, big // rows, piece, 0)
        return carry

    lax.fori_loop(0, matrix.shape[0] // big, block, 0)

    def finish(t, carry):
        copy(t).wait()
        return carry

    lax.fori_loop(0, blocks, finish, 0)
    for copy_of_part in whole:
        copy_of_part.wait()
    amp_copy.wait()


def shards(stem_mantissa, exponents, branch, closing, bitstrings):
    stem = stem_mantissa[0]
    k_local, r_all, q_local = stem.shape[1:]
    k_all, l_half = branch.shape[1:]
    l_all = 2 * l_half
    r_local = closing.shape[1]
    expo = jnp.transpose(exponents[0], (0, 2, 1))
    bits = bitstrings.reshape(1, -1)
    dma = pltpu.SemaphoreType.DMA
    hbm = pl.BlockSpec(memory_space=pl.ANY)
    vmem = pl.BlockSpec(memory_space=pltpu.VMEM)
    done, product, received, matrix, amps = pl.pallas_call(
        contract_kernel,
        out_shape=(
            pltpu.VMEM((2 * l_all, r_local, 128), BF16),
            pltpu.VMEM((2 * l_all * r_local, 128), F32),
            pltpu.VMEM((4, 2, k_all // 4, q_local), BF16),
            pltpu.VMEM((2 * l_all, 2 * k_all), BF16),
            jax.ShapeDtypeStruct((2, bits.shape[1]), F32),
        ),
        in_specs=[hbm] * 5,
        out_specs=(vmem, vmem, vmem, vmem, hbm),
        scratch_shapes=[
            pltpu.VMEM((SLOTS, 2, k_local, 16, 128), BF16),
            pltpu.VMEM(expo.shape, jnp.int32),
            pltpu.VMEM((2, k_local, r_all), F32),
            pltpu.VMEM((2, 256, 128), F32),
            pltpu.VMEM((8, 2, r_local, 2, k_local, q_local), BF16),
            pltpu.VMEM((r_local - 1, 4, 2, k_all // 4, q_local), BF16),
            pltpu.VMEM((2 * l_all * r_local, 128), F32),
            pltpu.VMEM((2, k_all, l_half), BF16),
            pltpu.VMEM((2, k_all, l_half), BF16),
            pltpu.VMEM((2, k_local, l_half), BF16),
            pltpu.VMEM((2, 8) + closing.shape, BF16),
            pltpu.VMEM((2, 8, 2, 2, r_local, 128), F32),
            pltpu.VMEM(bits.shape, jnp.int32),
            pltpu.VMEM((16, 1, 128), F32),
            pltpu.VMEM((16, 1, 128), F32),
            pltpu.VMEM((2, 1, 128), F32),
            pltpu.VMEM((8, 1, 128), F32),
            pltpu.VMEM((16, 1, 128), F32),
            pltpu.VMEM((2, bits.shape[1]), F32),
            dma((SLOTS,)), dma((2,)), dma,
            dma((2 * ROUNDS,)), dma((4 * ROUNDS,)),
            dma, dma, dma, dma, dma, dma, dma, dma, dma, dma, dma, dma, dma, dma, dma, dma, dma, dma,
            pltpu.SemaphoreType.REGULAR, pltpu.SemaphoreType.REGULAR,
        ],
        compiler_params=pltpu.CompilerParams(
            collective_id=0, has_side_effects=True, vmem_limit_bytes=34 * 2**20
        ),
        cost_estimate=pl.CostEstimate(
            flops=2 * (2 * k_all) * (2 * l_all) * r_local * q_local, bytes_accessed=2 * stem.size, transcendentals=0
        ),
        name="exchange_and_contract",
    )(stem, expo, branch, closing, bits)

    rows = 128
    big = 512
    keep_vmem = [pltpu.with_memory_space_constraint(a, pltpu.VMEM) for a in (done, product, received, matrix)]
    new_block, amps = pl.pallas_call(
        write_kernel,
        out_shape=(
            jax.ShapeDtypeStruct((2, l_all, r_local, q_local), BF16),
            jax.ShapeDtypeStruct(amps.shape, F32),
        ),
        in_specs=[vmem, vmem, vmem, vmem, hbm],
        out_specs=(hbm, hbm),
        scratch_shapes=[
            pltpu.VMEM((2 * l_all // rows, rows, r_local, 128), BF16),
            pltpu.VMEM((big * r_local, 128), F32),
            dma((2,)),
            dma((2 * l_all // rows,)),
            dma,
        ],
        compiler_params=pltpu.CompilerParams(vmem_limit_bytes=34 * 2**20),
        name="finish_and_write",
    )(*keep_vmem, amps)
    return (new_block[None], amps)


def solution(mesh):
    return jax.shard_map(
        shards,
        mesh=mesh,
        in_specs=(
            P("cuts", None, "idx", None, "br"),
            P("cuts", "idx", None, "br"),
            P(None, None, "br"),
            P(None, "idx", "br"),
            P(),
        ),
        out_specs=(P("cuts", None, None, "idx", "br"), P()),
        check_vma=False,
    )
```

```python
import jax
import jax.numpy as jnp
from jax import lax
from jax.experimental import pallas as pl
from jax.experimental.pallas import tpu as pltpu
from jax.sharding import PartitionSpec as P

MESH = pl.DeviceIdType.MESH
F32 = jnp.float32
BF16 = jnp.bfloat16
ROUNDS = 8
DEPTH = 2
SLOTS = 4


def full_wait(ref, sem):
    pltpu.make_async_copy(ref, ref, sem).wait()


def contract_kernel(
    stem, expo, branch, closing, bits,
    done, product, latest, matrix, amps,
    inbuf, raw_exp, scale, tiles, sendbuf, recvbuf, first, own_half, other_half, other_rows,
    env_raw, env, bits_v, part, part_in, mid, mid_in, total_in, amps_v,
    in_sem, small_sem, half_sem, send_sem, recv_sem, near_send, half_send, half_recv, fwd_send, fwd_recv,
    rows_send, rows_recv, env_send, env_recv, share_send, share_recv, part_send, part_recv, mid_send, mid_recv, total_send, total_recv, amp_sem,
    ready, twin_ready,
):
    c = lax.axis_index("cuts")
    me = lax.axis_index("idx")
    b = lax.axis_index("br")
    core = me % 2
    x = (me // 2) % 4
    z = me // 8
    k_local, q_local = sendbuf.shape[4:]

    def steps(n, sender):
        dz = (1 - (n // 2) % 2) % 2
        dx = (2 + n % 2) * (1 - n // 4) + (1 - n % 2) * (n // 4)
        return dz, dx * (1 + 2 * sender) % 4

    def group(n):
        dz, dx = steps(n, core)
        return ((z + dz) % 2) * 4 + (x + dx) % 4

    def source_group(n, sender):
        dz, dx = steps(n, sender)
        return ((z + dz) % 2) * 4 + (x + 4 - dx) % 4

    def peer(step):
        return (c, (me + step) % 16, b)

    rank = b * 4 + c

    def outer(q):
        return (q % 4, me, q // 4)

    twin = (c, (me + 8) % 16, 1 - b)
    sibling = (c, me + 1 - 2 * core, b)

    def load(step):
        rows = pl.ds(pl.multiple_of(group(step % 8) * 16, 16), 16)
        columns = pl.ds(pl.multiple_of((step // 8) * 128, 128), 128)
        slot = step % SLOTS
        return pltpu.make_async_copy(stem.at[:, :, rows, columns], inbuf.at[slot], in_sem.at[slot])

    exp_copy = pltpu.make_async_copy(expo, raw_exp, small_sem.at[0])
    exp_copy.start()
    for step in range(SLOTS):
        load(step).start()

    barrier = pltpu.get_barrier_semaphore()
    for step in range(1, 16):
        pl.semaphore_signal(barrier, inc=1, device_id=peer(step), device_id_type=MESH)

    @pl.when(b == 0)
    def _():
        pl.semaphore_signal(barrier, inc=1, device_id=twin, device_id_type=MESH)

    for q in range(1, 8):
        @pl.when(q > rank)
        def _(q=q):
            pl.semaphore_signal(barrier, inc=1, device_id=outer(q), device_id_type=MESH)

    bits_copy = pltpu.make_async_copy(bits, bits_v, small_sem.at[1])
    bits_copy.start()
    own_copy = pltpu.make_async_copy(branch, own_half, half_sem)
    own_copy.start()

    exp_copy.wait()
    for h in range(2):
        shifted = raw_exp[:, h, :] + 2
        low = (1 + shifted % 2).astype(F32)
        middle = (1 + 3 * ((shifted // 2) % 2)).astype(F32)
        high = (1 + 15 * ((shifted // 4) % 2)).astype(F32)
        scale[h] = 0.25 * low * middle * high

    def landing(n, dc, j, final):
        rows = pl.ds(pl.multiple_of((n % 4) * k_local, k_local), k_local)
        quarter = 2 * dc + n // 4
        return latest.at[quarter, :, rows, :] if final else recvbuf.at[j, quarter, :, rows, :]

    def message(n, dc, j, sem, final=False):
        cc = (core + dc) % 2
        return pltpu.make_async_remote_copy(
            src_ref=sendbuf.at[n, cc, j],
            dst_ref=landing(n, dc, j, final),
            send_sem=sem,
            recv_sem=recv_sem.at[4 * j + 2 * dc + n // 4],
            device_id=(c, group(n) * 2 + cc, b),
            device_id_type=MESH,
        )

    def keep(j, final=False):
        return pltpu.make_async_copy(sendbuf.at[7, core, j], landing(7, 0, j, final), recv_sem.at[4 * j + 1])

    def regroup(step):
        n = step % 8
        h = step // 8
        slot = step % SLOTS
        turn = (128 - group(n) * 16) % 128
        load(step).wait()

        def part_of_k(kb, carry):
            k0 = pl.multiple_of(kb * 16, 16)
            factors = pltpu.roll(scale[h, pl.ds(k0, 16), :], turn, 1)
            for p in range(2):
                tiles[p] = inbuf[slot, p, pl.ds(k0, 16)].astype(F32).reshape(256, 128)
            for r in range(16):
                factor = jnp.broadcast_to(factors[:, r:r + 1], (16, 128))
                spot = (r % 2) * 128
                for p in range(2):
                    rows = tiles[p, pl.ds(r, 16, stride=16), :] * factor
                    sendbuf[n, r // 8, 4 * h + r % 8 // 2, p, pl.ds(k0, 16), spot:spot + 128] = rows.astype(BF16)
            return carry

        lax.fori_loop(0, k_local // 16, part_of_k, 0)

    regroup(0)
    load(SLOTS).start()
    pl.semaphore_wait(barrier, 15 + rank + b)

    chip = me // 2

    def env_copy(step):
        return pltpu.make_async_remote_copy(
            src_ref=closing, dst_ref=env_raw.at[core, chip], send_sem=env_send, recv_sem=env_recv,
            device_id=peer(2 * step), device_id_type=MESH,
        )

    env_share = pltpu.make_async_remote_copy(
        src_ref=env_raw.at[core], dst_ref=env_raw.at[core], send_sem=share_send, recv_sem=share_recv,
        device_id=sibling, device_id_type=MESH,
    )

    half_rows = own_half.shape[1] // 2
    quarter = half_rows // 4

    def half_copy(t):
        rows = pl.ds(pl.multiple_of(core * half_rows + t * quarter, quarter), quarter)
        return pltpu.make_async_remote_copy(
            src_ref=branch.at[:, rows, :], dst_ref=other_half.at[:, rows, :],
            send_sem=half_send, recv_sem=half_recv, device_id=twin, device_id_type=MESH,
        )

    mine = pl.ds(pl.multiple_of(core * half_rows, half_rows), half_rows)
    theirs = pl.ds(pl.multiple_of((1 - core) * half_rows, half_rows), half_rows)
    forward = pltpu.make_async_remote_copy(
        src_ref=other_half.at[:, mine, :], dst_ref=other_half.at[:, mine, :],
        send_sem=fwd_send, recv_sem=fwd_recv, device_id=sibling, device_id_type=MESH,
    )
    twin_rows = pltpu.make_async_remote_copy(
        src_ref=branch.at[:, pl.ds(pl.multiple_of(((me + 8) % 16) * k_local, k_local), k_local), :],
        dst_ref=other_rows, send_sem=rows_send, recv_sem=rows_recv, device_id=twin, device_id_type=MESH,
    )


    @pl.when(b == 1)
    def _():
        pl.semaphore_signal(twin_ready, inc=1, device_id=twin, device_id_type=MESH)

    for q in range(7):
        @pl.when(q < rank)
        def _(q=q):
            pl.semaphore_signal(ready, inc=1, device_id=outer(q), device_id_type=MESH)

    message(0, 0, 0, send_sem.at[0]).start()
    message(0, 1, 0, send_sem.at[1]).start()
    for step in range(1, 8):
        env_copy(step).start()
    pltpu.make_async_copy(closing, env_raw.at[core, chip], env_recv).start()

    def produce(n, carry):
        regroup(n)
        load(n + SLOTS).start()
        message(n, 0, 0, send_sem.at[0]).start()
        message(n, 1, 0, send_sem.at[1]).start()

        return carry

    lax.fori_loop(1, 7, produce, 0)
    regroup(7)
    load(7 + SLOTS).start()
    keep(0).start()
    message(7, 1, 0, near_send).start()

    def issue(h, final=False):
        j = h // 2
        dc = h % 2

        def start(n, carry):
            message(n, dc, j, send_sem.at[h], final).start()
            return carry

        lax.fori_loop(0, 7, start, 0)

        @pl.when(dc == 0)
        def _():
            keep(j, final).start()

        @pl.when(dc == 1)
        def _():
            message(7, 1, j, near_send, final).start()

    def drained(h):
        full_wait(sendbuf.at[0, 0, pl.ds(0, 7)], send_sem.at[h])

    k_all = own_half.shape[1]
    l_half = own_half.shape[2]

    def fill(half, where):
        def step(kb, carry):
            quarter = kb // 2
            place = (quarter % 2) * 4 + (kb % 2) * 2
            row = pl.multiple_of(where * l_half, l_half)
            column = pl.multiple_of(quarter * (k_all // 2) + (kb % 2) * 128, 128)

            def turned(p):
                pieces = []
                for extra in (0, 1):
                    sender = (core + quarter // 2) % 2
                    source = 2 * source_group(place + extra, sender) + sender
                    pieces.append(half[p, pl.ds(pl.multiple_of(source * k_local, k_local), k_local), :])
                return jnp.concatenate(pieces, axis=0).T

            real = turned(0)
            imag = turned(1)
            matrix[pl.ds(row, l_half), pl.ds(column, 128)] = real
            matrix[pl.ds(row, l_half), pl.ds(k_all // 4 + column, 128)] = -imag
            matrix[pl.ds(2 * l_half + row, l_half), pl.ds(column, 128)] = imag
            matrix[pl.ds(2 * l_half + row, l_half), pl.ds(k_all // 4 + column, 128)] = real
            return carry

        lax.fori_loop(0, k_all // 128, step, 0)

    issue(2)

    @pl.when(b == 0)
    def _():
        pl.semaphore_wait(twin_ready, 1)

    twin_rows.start()
    for t in range(4):
        half_copy(t).start()

    def second_half(step, carry):
        regroup(step)

        @pl.when(step + SLOTS < 16)
        def _():
            load(step + SLOTS).start()

        return carry

    lax.fori_loop(8, 16, second_half, 0)
    full_wait(env_raw.at[core], env_recv)
    env_share.start()
    own_copy.wait()

    for h in range(4 - DEPTH):
        drained(h)
    issue(3)
    full_wait(env_raw.at[1 - core], share_recv)
    for h in range(2):
        env[:, :, :, h] = env_raw[:, :, :, :, h * 128:(h + 1) * 128].astype(F32)

    def gather_env(n, sums):
        g = group(n)

        def row(t, sums):
            cc = t // 4
            pair = t % 4
            new = list(sums)
            for h in range(2):
                for p in range(2):
                    values = sendbuf[n, cc, 4 * h + pair, p].astype(F32)
                    for e in range(2):
                        for s in range(2):
                            weight = env[cc, g, e, h, pl.ds(2 * pair + s, 1), :]
                            new[2 * p + e] = new[2 * p + e] + values[:, s * 128:(s + 1) * 128] * weight
            return tuple(new)

        return lax.fori_loop(0, 8, row, sums)

    zero = jnp.zeros((k_local, 128), F32)
    sums = lax.fori_loop(0, 8, gather_env, (zero,) * 4)
    w = [jnp.sum(s, axis=1, keepdims=True) for s in sums]
    w_real = w[0] - w[3]
    w_imag = w[1] + w[2]

    k_mine = pl.ds(pl.multiple_of(me * k_local, k_local), k_local)
    blocks = l_half // 128
    full_wait(other_rows, rows_recv)
    for half, rows, where in ((own_half, k_mine, b), (other_rows, slice(None), 1 - b)):
        real = half[0, rows, :].astype(F32)
        imag = half[1, rows, :].astype(F32)
        closed_real = jnp.sum(real * w_real - imag * w_imag, axis=0, keepdims=True)
        closed_imag = jnp.sum(real * w_imag + imag * w_real, axis=0, keepdims=True)
        for t in range(blocks):
            part[where * blocks + t] = closed_real[:, t * 128:(t + 1) * 128]
            part[2 * blocks + where * blocks + t] = closed_imag[:, t * 128:(t + 1) * 128]

    def part_copy(step):
        to = (me + step) % 16
        return pltpu.make_async_remote_copy(
            src_ref=part.at[to], dst_ref=part_in.at[me], send_sem=part_send, recv_sem=part_recv,
            device_id=(c, to, b), device_id_type=MESH,
        )

    def mid_copy(q):
        return pltpu.make_async_remote_copy(
            src_ref=mid.at[0], dst_ref=mid_in.at[rank], send_sem=mid_send, recv_sem=mid_recv,
            device_id=outer(q), device_id_type=MESH,
        )

    def total_copy(step):
        return pltpu.make_async_remote_copy(
            src_ref=mid.at[1], dst_ref=total_in.at[me], send_sem=total_send, recv_sem=total_recv,
            device_id=peer(step), device_id_type=MESH,
        )

    for step in range(1, 16):
        part_copy(step).start()
    pltpu.make_async_copy(part.at[me], part_in.at[me], part_recv).start()

    drained(4 - DEPTH)
    issue(4)
    fill(own_half, b)

    drained(5 - DEPTH)
    issue(5)
    full_wait(part_in, part_recv)
    mid[0] = jnp.sum(part_in[...], axis=0)

    @pl.when(rank < 7)
    def _():
        pl.semaphore_wait(ready, 7 - rank)

    for q in range(8):
        @pl.when(q != rank)
        def _(q=q):
            mid_copy(q).start()

    pltpu.make_async_copy(mid.at[0], mid_in.at[rank], mid_recv).start()

    drained(6 - DEPTH)
    issue(6)
    full_wait(other_half.at[:, mine, :], half_recv)
    forward.start()
    full_wait(mid_in, mid_recv)
    mid[1] = jnp.sum(mid_in[...], axis=0)
    for step in range(1, 16):
        total_copy(step).start()
    pltpu.make_async_copy(mid.at[1], total_in.at[me], total_recv).start()

    drained(7 - DEPTH)
    issue(7)
    full_wait(other_half.at[:, theirs, :], fwd_recv)
    fill(other_half, 1 - b)

    drained(8 - DEPTH)
    issue(8)

    def choose():
        full_wait(total_in, total_recv)
        bits_copy.wait()
        chosen = bits_v[...]
        found = jnp.zeros((8, chosen.shape[1]), F32)
        for t in range(2 * blocks):
            rows = [total_in[t], total_in[2 * blocks + t], jnp.zeros((6, 128), F32)]
            spots = lax.broadcasted_iota(jnp.int32, (128, chosen.shape[1]), 0) + t * 128
            pick = jnp.where(spots == chosen, 1.0, 0.0).astype(F32)
            found = found + jnp.dot(
                jnp.concatenate(rows, axis=0), pick, precision=lax.Precision.HIGHEST, preferred_element_type=F32
            )
        amps_v[...] = found[:2]
        pltpu.make_async_copy(amps_v, amps, amp_sem).start()

    m_block = 512

    def tile_rows(m0, j, s):
        return pl.ds(m0 * ROUNDS + 2 * (j % 4) + s, m_block, stride=ROUNDS)

    def chunk(target):
        def run(j, carry):
            drained(j + 9 - DEPTH)

            @pl.when(j + 9 < 2 * ROUNDS - 2)
            def _():
                issue(j + 9)

            @pl.when(j + 9 >= 2 * ROUNDS - 2)
            def _():
                issue(j + 9, True)

            for quarter in range(4):
                full_wait(recvbuf.at[j, quarter], recv_sem.at[4 * j + quarter])

            def rows(m, carry):
                m0 = pl.multiple_of(m * m_block, m_block)
                right = recvbuf[j].reshape(2 * k_all, q_local)
                result = jnp.dot(matrix[pl.ds(m0, m_block), :], right, preferred_element_type=F32)
                for s in range(2):
                    target[tile_rows(m0, j, s), :] = result[:, s * 128:(s + 1) * 128]
                return carry

            lax.fori_loop(0, matrix.shape[0] // m_block, rows, 0)

            @pl.when(j == 2)
            def _():
                choose()

            return carry

        return run

    lax.fori_loop(0, ROUNDS // 2, chunk(first), 0)

    def settle(t, carry):
        t0 = pl.multiple_of(t * 128, 128)
        block = first[pl.ds(pl.multiple_of(t0 * ROUNDS, 128 * ROUNDS), 128 * ROUNDS), :]
        done[pl.ds(t0, 128)] = block.reshape(128, ROUNDS, 128).astype(BF16)
        return carry

    lax.fori_loop(0, matrix.shape[0] // 128, settle, 0)
    lax.fori_loop(ROUNDS // 2, ROUNDS - 1, chunk(product), 0)

    def early(low, high):
        columns = slice(low * (k_all // 2), high * (k_all // 2))

        def rows(m, carry):
            m0 = pl.multiple_of(m * m_block, m_block)
            right = latest[low:high].reshape((high - low) * (k_all // 2), q_local)
            result = jnp.dot(matrix[pl.ds(m0, m_block), columns], right, preferred_element_type=F32)
            for s in range(2):
                spots = tile_rows(m0, ROUNDS - 1, s)
                piece = result[:, s * 128:(s + 1) * 128]
                product[spots, :] = piece if low == 0 else product[spots, :] + piece
            return carry

        lax.fori_loop(0, matrix.shape[0] // m_block, rows, 0)

    last = 4 * (ROUNDS - 1)
    full_wait(latest.at[0], recv_sem.at[last])
    full_wait(latest.at[1], recv_sem.at[last + 1])
    early(0, 2)
    full_wait(latest.at[2], recv_sem.at[last + 2])
    full_wait(latest.at[3], recv_sem.at[last + 3])

    for h in range(2 * ROUNDS - DEPTH, 2 * ROUNDS):
        drained(h)
    full_wait(sendbuf.at[7, 0], near_send)
    full_wait(other_rows, rows_send)
    full_wait(env_raw.at[core], share_send)
    full_wait(other_half.at[:, mine, :], half_send)
    full_wait(other_half.at[:, mine, :], fwd_send)
    full_wait(env_raw.at[0, pl.ds(0, 7)], env_send)
    full_wait(part_in.at[pl.ds(0, 15)], part_send)
    full_wait(mid_in.at[pl.ds(0, 7)], mid_send)
    full_wait(total_in.at[pl.ds(0, 15)], total_send)
    full_wait(amps_v, amp_sem)


def write_kernel(
    done, product, latest, matrix, amps_in, out, amps, staging, spread, done_sem, out_sem, amp_sem
):
    amp_copy = pltpu.make_async_copy(amps_in, amps, amp_sem)
    amp_copy.start()
    blocks, rows = staging.shape[:2]
    l_all = out.shape[1]
    per_part = l_all // rows
    quarter = matrix.shape[1] // 4
    big = spread.shape[0] // ROUNDS
    whole = [
        pltpu.make_async_copy(done.at[pl.ds(p * l_all, l_all)], out.at[p, :, :, pl.ds(0, 128)], done_sem.at[p])
        for p in range(2)
    ]
    for copy in whole:
        copy.start()

    def copy(t):
        return pltpu.make_async_copy(
            staging.at[t],
            out.at[t // per_part, pl.ds((t % per_part) * rows, rows), :, pl.ds(128, 128)],
            out_sem.at[t],
        )

    def block(m, carry):
        m0 = pl.multiple_of(m * big, big)
        right = latest[2:].reshape(2 * quarter, latest.shape[3])
        result = jnp.dot(matrix[pl.ds(m0, big), 2 * quarter:], right, preferred_element_type=F32)
        for s in range(2):
            spread[pl.ds(ROUNDS - 2 + s, big, stride=ROUNDS), :] = result[:, s * 128:(s + 1) * 128]

        def piece(i, carry):
            t = m * (big // rows) + i
            spots = pl.ds(pl.multiple_of(t * rows * ROUNDS, rows * ROUNDS), rows * ROUNDS)
            local = pl.ds(pl.multiple_of(i * rows * ROUNDS, rows * ROUNDS), rows * ROUNDS)
            before = product[spots, :].reshape(rows, ROUNDS, 128)
            newest = spread[local, :].reshape(rows, ROUNDS, 128)
            spot = lax.broadcasted_iota(jnp.int32, (rows, ROUNDS, 128), 1)
            staging[t] = (before + jnp.where(spot >= ROUNDS - 2, newest, 0.0)).astype(BF16)
            copy(t).start()
            return carry

        lax.fori_loop(0, big // rows, piece, 0)
        return carry

    lax.fori_loop(0, matrix.shape[0] // big, block, 0)

    def finish(t, carry):
        copy(t).wait()
        return carry

    lax.fori_loop(0, blocks, finish, 0)
    for copy_of_part in whole:
        copy_of_part.wait()
    amp_copy.wait()


def shards(stem_mantissa, exponents, branch, closing, bitstrings):
    stem = stem_mantissa[0]
    k_local, r_all, q_local = stem.shape[1:]
    k_all, l_half = branch.shape[1:]
    l_all = 2 * l_half
    r_local = closing.shape[1]
    expo = jnp.transpose(exponents[0], (0, 2, 1))
    bits = bitstrings.reshape(1, -1)
    dma = pltpu.SemaphoreType.DMA
    hbm = pl.BlockSpec(memory_space=pl.ANY)
    vmem = pl.BlockSpec(memory_space=pltpu.VMEM)
    done, product, received, matrix, amps = pl.pallas_call(
        contract_kernel,
        out_shape=(
            pltpu.VMEM((2 * l_all, r_local, 128), BF16),
            pltpu.VMEM((2 * l_all * r_local, 128), F32),
            pltpu.VMEM((4, 2, k_all // 4, q_local), BF16),
            pltpu.VMEM((2 * l_all, 2 * k_all), BF16),
            jax.ShapeDtypeStruct((2, bits.shape[1]), F32),
        ),
        in_specs=[hbm] * 5,
        out_specs=(vmem, vmem, vmem, vmem, hbm),
        scratch_shapes=[
            pltpu.VMEM((SLOTS, 2, k_local, 16, 128), BF16),
            pltpu.VMEM(expo.shape, jnp.int32),
            pltpu.VMEM((2, k_local, r_all), F32),
            pltpu.VMEM((2, 256, 128), F32),
            pltpu.VMEM((8, 2, r_local, 2, k_local, q_local), BF16),
            pltpu.VMEM((r_local - 1, 4, 2, k_all // 4, q_local), BF16),
            pltpu.VMEM((2 * l_all * r_local, 128), F32),
            pltpu.VMEM((2, k_all, l_half), BF16),
            pltpu.VMEM((2, k_all, l_half), BF16),
            pltpu.VMEM((2, k_local, l_half), BF16),
            pltpu.VMEM((2, 8) + closing.shape, BF16),
            pltpu.VMEM((2, 8, 2, 2, r_local, 128), F32),
            pltpu.VMEM(bits.shape, jnp.int32),
            pltpu.VMEM((16, 1, 128), F32),
            pltpu.VMEM((16, 1, 128), F32),
            pltpu.VMEM((2, 1, 128), F32),
            pltpu.VMEM((8, 1, 128), F32),
            pltpu.VMEM((16, 1, 128), F32),
            pltpu.VMEM((2, bits.shape[1]), F32),
            dma((SLOTS,)), dma((2,)), dma,
            dma((2 * ROUNDS,)), dma((4 * ROUNDS,)),
            dma, dma, dma, dma, dma, dma, dma, dma, dma, dma, dma, dma, dma, dma, dma, dma, dma, dma,
            pltpu.SemaphoreType.REGULAR, pltpu.SemaphoreType.REGULAR,
        ],
        compiler_params=pltpu.CompilerParams(
            collective_id=0, has_side_effects=True, vmem_limit_bytes=34 * 2**20
        ),
        cost_estimate=pl.CostEstimate(
            flops=2 * (2 * k_all) * (2 * l_all) * r_local * q_local, bytes_accessed=2 * stem.size, transcendentals=0
        ),
        name="exchange_and_contract",
    )(stem, expo, branch, closing, bits)

    rows = 128
    big = 512
    keep_vmem = [pltpu.with_memory_space_constraint(a, pltpu.VMEM) for a in (done, product, received, matrix)]
    new_block, amps = pl.pallas_call(
        write_kernel,
        out_shape=(
            jax.ShapeDtypeStruct((2, l_all, r_local, q_local), BF16),
            jax.ShapeDtypeStruct(amps.shape, F32),
        ),
        in_specs=[vmem, vmem, vmem, vmem, hbm],
        out_specs=(hbm, hbm),
        scratch_shapes=[
            pltpu.VMEM((2 * l_all // rows, rows, r_local, 128), BF16),
            pltpu.VMEM((big * r_local, 128), F32),
            dma((2,)),
            dma((2 * l_all // rows,)),
            dma,
        ],
        compiler_params=pltpu.CompilerParams(vmem_limit_bytes=34 * 2**20),
        name="finish_and_write",
    )(*keep_vmem, amps)
    return (new_block[None], amps)


def solution(mesh):
    return jax.shard_map(
        shards,
        mesh=mesh,
        in_specs=(
            P("cuts", None, "idx", None, "br"),
            P("cuts", "idx", None, "br"),
            P(None, None, "br"),
            P(None, "idx", "br"),
            P(),
        ),
        out_specs=(P("cuts", None, None, "idx", "br"), P()),
        check_vma=False,
    )
```

```python
import jax
import jax.numpy as jnp
from jax import lax
from jax.experimental import pallas as pl
from jax.experimental.pallas import tpu as pltpu
from jax.sharding import PartitionSpec as P

MESH = pl.DeviceIdType.MESH
F32 = jnp.float32
BF16 = jnp.bfloat16
ROUNDS = 8
DEPTH = 2
SLOTS = 4


def full_wait(ref, sem):
    pltpu.make_async_copy(ref, ref, sem).wait()


def contract_kernel(
    stem, expo, branch, closing, bits,
    done, product, latest, matrix, amps,
    inbuf, raw_exp, scale, tiles, sendbuf, recvbuf, first, own_half, other_half, other_rows,
    env_raw, env, bits_v, part, part_in, mid, mid_in, total_in, amps_v,
    in_sem, small_sem, half_sem, send_sem, recv_sem, near_send, half_send, half_recv, fwd_send, fwd_recv,
    rows_send, rows_recv, env_send, env_recv, share_send, share_recv, part_send, part_recv, mid_send, mid_recv, total_send, total_recv, amp_sem,
    ready, twin_ready,
):
    c = lax.axis_index("cuts")
    me = lax.axis_index("idx")
    b = lax.axis_index("br")
    core = me % 2
    x = (me // 2) % 4
    z = me // 8
    k_local, q_local = sendbuf.shape[4:]

    def steps(n, sender):
        dz = (1 - (n // 2) % 2) % 2
        dx = (2 + n % 2) * (1 - n // 4) + (1 - n % 2) * (n // 4)
        return dz, dx * (1 + 2 * sender) % 4

    def group(n):
        dz, dx = steps(n, core)
        return ((z + dz) % 2) * 4 + (x + dx) % 4

    def source_group(n, sender):
        dz, dx = steps(n, sender)
        return ((z + dz) % 2) * 4 + (x + 4 - dx) % 4

    def peer(step):
        return (c, (me + step) % 16, b)

    rank = b * 4 + c

    def outer(q):
        return (q % 4, me, q // 4)

    twin = (c, (me + 8) % 16, 1 - b)
    sibling = (c, me + 1 - 2 * core, b)

    def load(step):
        rows = pl.ds(pl.multiple_of(group(step % 8) * 16, 16), 16)
        columns = pl.ds(pl.multiple_of((step // 8) * 128, 128), 128)
        slot = step % SLOTS
        return pltpu.make_async_copy(stem.at[:, :, rows, columns], inbuf.at[slot], in_sem.at[slot])

    exp_copy = pltpu.make_async_copy(expo, raw_exp, small_sem.at[0])
    exp_copy.start()
    for step in range(SLOTS):
        load(step).start()

    barrier = pltpu.get_barrier_semaphore()
    for step in range(1, 16):
        pl.semaphore_signal(barrier, inc=1, device_id=peer(step), device_id_type=MESH)

    @pl.when(b == 0)
    def _():
        pl.semaphore_signal(barrier, inc=1, device_id=twin, device_id_type=MESH)

    for q in range(1, 8):
        @pl.when(q > rank)
        def _(q=q):
            pl.semaphore_signal(barrier, inc=1, device_id=outer(q), device_id_type=MESH)

    bits_copy = pltpu.make_async_copy(bits, bits_v, small_sem.at[1])
    bits_copy.start()
    own_copy = pltpu.make_async_copy(branch, own_half, half_sem)
    own_copy.start()

    exp_copy.wait()
    for h in range(2):
        shifted = raw_exp[:, h, :] + 2
        low = (1 + shifted % 2).astype(F32)
        middle = (1 + 3 * ((shifted // 2) % 2)).astype(F32)
        high = (1 + 15 * ((shifted // 4) % 2)).astype(F32)
        scale[h] = 0.25 * low * middle * high

    def landing(n, dc, j, final):
        rows = pl.ds(pl.multiple_of((n % 4) * k_local, k_local), k_local)
        quarter = 2 * dc + n // 4
        return latest.at[quarter, :, rows, :] if final else recvbuf.at[j, quarter, :, rows, :]

    def message(n, dc, j, sem, final=False):
        cc = (core + dc) % 2
        return pltpu.make_async_remote_copy(
            src_ref=sendbuf.at[n, cc, j],
            dst_ref=landing(n, dc, j, final),
            send_sem=sem,
            recv_sem=recv_sem.at[4 * j + 2 * dc + n // 4],
            device_id=(c, group(n) * 2 + cc, b),
            device_id_type=MESH,
        )

    def keep(j, final=False):
        return pltpu.make_async_copy(sendbuf.at[7, core, j], landing(7, 0, j, final), recv_sem.at[4 * j + 1])

    def regroup(step):
        n = step % 8
        h = step // 8
        slot = step % SLOTS
        turn = (128 - group(n) * 16) % 128
        load(step).wait()

        def part_of_k(kb, carry):
            k0 = pl.multiple_of(kb * 16, 16)
            factors = pltpu.roll(scale[h, pl.ds(k0, 16), :], turn, 1)
            for p in range(2):
                tiles[p] = inbuf[slot, p, pl.ds(k0, 16)].astype(F32).reshape(256, 128)
            for r in range(16):
                factor = jnp.broadcast_to(factors[:, r:r + 1], (16, 128))
                spot = (r % 2) * 128
                for p in range(2):
                    rows = tiles[p, pl.ds(r, 16, stride=16), :] * factor
                    sendbuf[n, r // 8, 4 * h + r % 8 // 2, p, pl.ds(k0, 16), spot:spot + 128] = rows.astype(BF16)
            return carry

        lax.fori_loop(0, k_local // 16, part_of_k, 0)

    regroup(0)
    load(SLOTS).start()
    pl.semaphore_wait(barrier, 15 + rank + b)

    chip = me // 2

    def env_copy(step):
        return pltpu.make_async_remote_copy(
            src_ref=closing, dst_ref=env_raw.at[core, chip], send_sem=env_send, recv_sem=env_recv,
            device_id=peer(2 * step), device_id_type=MESH,
        )

    env_share = pltpu.make_async_remote_copy(
        src_ref=env_raw.at[core], dst_ref=env_raw.at[core], send_sem=share_send, recv_sem=share_recv,
        device_id=sibling, device_id_type=MESH,
    )

    half_rows = own_half.shape[1] // 2
    quarter = half_rows // 4

    def half_copy(t):
        rows = pl.ds(pl.multiple_of(core * half_rows + t * quarter, quarter), quarter)
        return pltpu.make_async_remote_copy(
            src_ref=branch.at[:, rows, :], dst_ref=other_half.at[:, rows, :],
            send_sem=half_send, recv_sem=half_recv, device_id=twin, device_id_type=MESH,
        )

    mine = pl.ds(pl.multiple_of(core * half_rows, half_rows), half_rows)
    theirs = pl.ds(pl.multiple_of((1 - core) * half_rows, half_rows), half_rows)
    forward = pltpu.make_async_remote_copy(
        src_ref=other_half.at[:, mine, :], dst_ref=other_half.at[:, mine, :],
        send_sem=fwd_send, recv_sem=fwd_recv, device_id=sibling, device_id_type=MESH,
    )
    twin_rows = pltpu.make_async_remote_copy(
        src_ref=branch.at[:, pl.ds(pl.multiple_of(((me + 8) % 16) * k_local, k_local), k_local), :],
        dst_ref=other_rows, send_sem=rows_send, recv_sem=rows_recv, device_id=twin, device_id_type=MESH,
    )


    @pl.when(b == 1)
    def _():
        pl.semaphore_signal(twin_ready, inc=1, device_id=twin, device_id_type=MESH)

    for q in range(7):
        @pl.when(q < rank)
        def _(q=q):
            pl.semaphore_signal(ready, inc=1, device_id=outer(q), device_id_type=MESH)

    message(0, 0, 0, send_sem.at[0]).start()
    message(0, 1, 0, send_sem.at[1]).start()

    def produce(n, carry):
        regroup(n)
        load(n + SLOTS).start()
        message(n, 0, 0, send_sem.at[0]).start()
        message(n, 1, 0, send_sem.at[1]).start()

        return carry

    lax.fori_loop(1, 7, produce, 0)
    regroup(7)
    load(7 + SLOTS).start()
    keep(0).start()
    message(7, 1, 0, near_send).start()
    for step in range(1, 8):
        env_copy(step).start()
    pltpu.make_async_copy(closing, env_raw.at[core, chip], env_recv).start()

    def issue(h, final=False):
        j = h // 2
        dc = h % 2

        def start(n, carry):
            message(n, dc, j, send_sem.at[h], final).start()
            return carry

        lax.fori_loop(0, 7, start, 0)

        @pl.when(dc == 0)
        def _():
            keep(j, final).start()

        @pl.when(dc == 1)
        def _():
            message(7, 1, j, near_send, final).start()

    def drained(h):
        full_wait(sendbuf.at[0, 0, pl.ds(0, 7)], send_sem.at[h])

    k_all = own_half.shape[1]
    l_half = own_half.shape[2]

    def fill(half, where):
        def step(kb, carry):
            quarter = kb // 2
            place = (quarter % 2) * 4 + (kb % 2) * 2
            row = pl.multiple_of(where * l_half, l_half)
            column = pl.multiple_of(quarter * (k_all // 2) + (kb % 2) * 128, 128)

            def turned(p):
                pieces = []
                for extra in (0, 1):
                    sender = (core + quarter // 2) % 2
                    source = 2 * source_group(place + extra, sender) + sender
                    pieces.append(half[p, pl.ds(pl.multiple_of(source * k_local, k_local), k_local), :])
                return jnp.concatenate(pieces, axis=0).T

            real = turned(0)
            imag = turned(1)
            matrix[pl.ds(row, l_half), pl.ds(column, 128)] = real
            matrix[pl.ds(row, l_half), pl.ds(k_all // 4 + column, 128)] = -imag
            matrix[pl.ds(2 * l_half + row, l_half), pl.ds(column, 128)] = imag
            matrix[pl.ds(2 * l_half + row, l_half), pl.ds(k_all // 4 + column, 128)] = real
            return carry

        lax.fori_loop(0, k_all // 128, step, 0)

    issue(2)

    @pl.when(b == 0)
    def _():
        pl.semaphore_wait(twin_ready, 1)

    twin_rows.start()
    for t in range(4):
        half_copy(t).start()

    def second_half(step, carry):
        regroup(step)

        @pl.when(step + SLOTS < 16)
        def _():
            load(step + SLOTS).start()

        return carry

    lax.fori_loop(8, 16, second_half, 0)
    full_wait(env_raw.at[core], env_recv)
    env_share.start()
    own_copy.wait()

    for h in range(4 - DEPTH):
        drained(h)
    issue(3)
    full_wait(env_raw.at[1 - core], share_recv)
    for h in range(2):
        env[:, :, :, h] = env_raw[:, :, :, :, h * 128:(h + 1) * 128].astype(F32)

    def gather_env(n, sums):
        g = group(n)

        def row(t, sums):
            cc = t // 4
            pair = t % 4
            new = list(sums)
            for h in range(2):
                for p in range(2):
                    values = sendbuf[n, cc, 4 * h + pair, p].astype(F32)
                    for e in range(2):
                        for s in range(2):
                            weight = env[cc, g, e, h, pl.ds(2 * pair + s, 1), :]
                            new[2 * p + e] = new[2 * p + e] + values[:, s * 128:(s + 1) * 128] * weight
            return tuple(new)

        return lax.fori_loop(0, 8, row, sums)

    zero = jnp.zeros((k_local, 128), F32)
    sums = lax.fori_loop(0, 8, gather_env, (zero,) * 4)
    w = [jnp.sum(s, axis=1, keepdims=True) for s in sums]
    w_real = w[0] - w[3]
    w_imag = w[1] + w[2]

    k_mine = pl.ds(pl.multiple_of(me * k_local, k_local), k_local)
    blocks = l_half // 128
    full_wait(other_rows, rows_recv)
    for half, rows, where in ((own_half, k_mine, b), (other_rows, slice(None), 1 - b)):
        real = half[0, rows, :].astype(F32)
        imag = half[1, rows, :].astype(F32)
        closed_real = jnp.sum(real * w_real - imag * w_imag, axis=0, keepdims=True)
        closed_imag = jnp.sum(real * w_imag + imag * w_real, axis=0, keepdims=True)
        for t in range(blocks):
            part[where * blocks + t] = closed_real[:, t * 128:(t + 1) * 128]
            part[2 * blocks + where * blocks + t] = closed_imag[:, t * 128:(t + 1) * 128]

    def part_copy(step):
        to = (me + step) % 16
        return pltpu.make_async_remote_copy(
            src_ref=part.at[to], dst_ref=part_in.at[me], send_sem=part_send, recv_sem=part_recv,
            device_id=(c, to, b), device_id_type=MESH,
        )

    def mid_copy(q):
        return pltpu.make_async_remote_copy(
            src_ref=mid.at[0], dst_ref=mid_in.at[rank], send_sem=mid_send, recv_sem=mid_recv,
            device_id=outer(q), device_id_type=MESH,
        )

    def total_copy(step):
        return pltpu.make_async_remote_copy(
            src_ref=mid.at[1], dst_ref=total_in.at[me], send_sem=total_send, recv_sem=total_recv,
            device_id=peer(step), device_id_type=MESH,
        )

    for step in range(1, 16):
        part_copy(step).start()
    pltpu.make_async_copy(part.at[me], part_in.at[me], part_recv).start()

    drained(4 - DEPTH)
    issue(4)
    fill(own_half, b)

    drained(5 - DEPTH)
    issue(5)
    full_wait(part_in, part_recv)
    mid[0] = jnp.sum(part_in[...], axis=0)

    @pl.when(rank < 7)
    def _():
        pl.semaphore_wait(ready, 7 - rank)

    for q in range(8):
        @pl.when(q != rank)
        def _(q=q):
            mid_copy(q).start()

    pltpu.make_async_copy(mid.at[0], mid_in.at[rank], mid_recv).start()

    drained(6 - DEPTH)
    issue(6)
    full_wait(other_half.at[:, mine, :], half_recv)
    forward.start()
    full_wait(mid_in, mid_recv)
    mid[1] = jnp.sum(mid_in[...], axis=0)
    for step in range(1, 16):
        total_copy(step).start()
    pltpu.make_async_copy(mid.at[1], total_in.at[me], total_recv).start()

    drained(7 - DEPTH)
    issue(7)
    full_wait(other_half.at[:, theirs, :], fwd_recv)
    fill(other_half, 1 - b)

    drained(8 - DEPTH)
    issue(8)

    def choose():
        full_wait(total_in, total_recv)
        bits_copy.wait()
        chosen = bits_v[...]
        found = jnp.zeros((8, chosen.shape[1]), F32)
        for t in range(2 * blocks):
            rows = [total_in[t], total_in[2 * blocks + t], jnp.zeros((6, 128), F32)]
            spots = lax.broadcasted_iota(jnp.int32, (128, chosen.shape[1]), 0) + t * 128
            pick = jnp.where(spots == chosen, 1.0, 0.0).astype(F32)
            found = found + jnp.dot(
                jnp.concatenate(rows, axis=0), pick, precision=lax.Precision.HIGHEST, preferred_element_type=F32
            )
        amps_v[...] = found[:2]
        pltpu.make_async_copy(amps_v, amps, amp_sem).start()

    m_block = 512

    def tile_rows(m0, j, s):
        return pl.ds(m0 * ROUNDS + 2 * (j % 4) + s, m_block, stride=ROUNDS)

    def chunk(target):
        def run(j, carry):
            drained(j + 9 - DEPTH)

            @pl.when(j + 9 < 2 * ROUNDS - 2)
            def _():
                issue(j + 9)

            @pl.when(j + 9 >= 2 * ROUNDS - 2)
            def _():
                issue(j + 9, True)

            for quarter in range(4):
                full_wait(recvbuf.at[j, quarter], recv_sem.at[4 * j + quarter])

            def rows(m, carry):
                m0 = pl.multiple_of(m * m_block, m_block)
                right = recvbuf[j].reshape(2 * k_all, q_local)
                result = jnp.dot(matrix[pl.ds(m0, m_block), :], right, preferred_element_type=F32)
                for s in range(2):
                    target[tile_rows(m0, j, s), :] = result[:, s * 128:(s + 1) * 128]
                return carry

            lax.fori_loop(0, matrix.shape[0] // m_block, rows, 0)

            @pl.when(j == 2)
            def _():
                choose()

            return carry

        return run

    lax.fori_loop(0, ROUNDS // 2, chunk(first), 0)

    def settle(t, carry):
        t0 = pl.multiple_of(t * 128, 128)
        block = first[pl.ds(pl.multiple_of(t0 * ROUNDS, 128 * ROUNDS), 128 * ROUNDS), :]
        done[pl.ds(t0, 128)] = block.reshape(128, ROUNDS, 128).astype(BF16)
        return carry

    lax.fori_loop(0, matrix.shape[0] // 128, settle, 0)
    lax.fori_loop(ROUNDS // 2, ROUNDS - 1, chunk(product), 0)

    def early(low, high):
        columns = slice(low * (k_all // 2), high * (k_all // 2))

        def rows(m, carry):
            m0 = pl.multiple_of(m * m_block, m_block)
            right = latest[low:high].reshape((high - low) * (k_all // 2), q_local)
            result = jnp.dot(matrix[pl.ds(m0, m_block), columns], right, preferred_element_type=F32)
            for s in range(2):
                spots = tile_rows(m0, ROUNDS - 1, s)
                piece = result[:, s * 128:(s + 1) * 128]
                product[spots, :] = piece if low == 0 else product[spots, :] + piece
            return carry

        lax.fori_loop(0, matrix.shape[0] // m_block, rows, 0)

    last = 4 * (ROUNDS - 1)
    full_wait(latest.at[0], recv_sem.at[last])
    full_wait(latest.at[1], recv_sem.at[last + 1])
    early(0, 2)
    full_wait(latest.at[2], recv_sem.at[last + 2])
    full_wait(latest.at[3], recv_sem.at[last + 3])

    for h in range(2 * ROUNDS - DEPTH, 2 * ROUNDS):
        drained(h)
    full_wait(sendbuf.at[7, 0], near_send)
    full_wait(other_rows, rows_send)
    full_wait(env_raw.at[core], share_send)
    full_wait(other_half.at[:, mine, :], half_send)
    full_wait(other_half.at[:, mine, :], fwd_send)
    full_wait(env_raw.at[0, pl.ds(0, 7)], env_send)
    full_wait(part_in.at[pl.ds(0, 15)], part_send)
    full_wait(mid_in.at[pl.ds(0, 7)], mid_send)
    full_wait(total_in.at[pl.ds(0, 15)], total_send)
    full_wait(amps_v, amp_sem)


def write_kernel(
    done, product, latest, matrix, amps_in, out, amps, staging, spread, done_sem, out_sem, amp_sem
):
    amp_copy = pltpu.make_async_copy(amps_in, amps, amp_sem)
    amp_copy.start()
    blocks, rows = staging.shape[:2]
    l_all = out.shape[1]
    per_part = l_all // rows
    quarter = matrix.shape[1] // 4
    big = spread.shape[0] // ROUNDS
    whole = [
        pltpu.make_async_copy(done.at[pl.ds(p * l_all, l_all)], out.at[p, :, :, pl.ds(0, 128)], done_sem.at[p])
        for p in range(2)
    ]
    for copy in whole:
        copy.start()

    def copy(t):
        return pltpu.make_async_copy(
            staging.at[t],
            out.at[t // per_part, pl.ds((t % per_part) * rows, rows), :, pl.ds(128, 128)],
            out_sem.at[t],
        )

    def block(m, carry):
        m0 = pl.multiple_of(m * big, big)
        right = latest[2:].reshape(2 * quarter, latest.shape[3])
        result = jnp.dot(matrix[pl.ds(m0, big), 2 * quarter:], right, preferred_element_type=F32)
        for s in range(2):
            spread[pl.ds(ROUNDS - 2 + s, big, stride=ROUNDS), :] = result[:, s * 128:(s + 1) * 128]

        def piece(i, carry):
            t = m * (big // rows) + i
            spots = pl.ds(pl.multiple_of(t * rows * ROUNDS, rows * ROUNDS), rows * ROUNDS)
            local = pl.ds(pl.multiple_of(i * rows * ROUNDS, rows * ROUNDS), rows * ROUNDS)
            before = product[spots, :].reshape(rows, ROUNDS, 128)
            newest = spread[local, :].reshape(rows, ROUNDS, 128)
            spot = lax.broadcasted_iota(jnp.int32, (rows, ROUNDS, 128), 1)
            staging[t] = (before + jnp.where(spot >= ROUNDS - 2, newest, 0.0)).astype(BF16)
            copy(t).start()
            return carry

        lax.fori_loop(0, big // rows, piece, 0)
        return carry

    lax.fori_loop(0, matrix.shape[0] // big, block, 0)

    def finish(t, carry):
        copy(t).wait()
        return carry

    lax.fori_loop(0, blocks, finish, 0)
    for copy_of_part in whole:
        copy_of_part.wait()
    amp_copy.wait()


def shards(stem_mantissa, exponents, branch, closing, bitstrings):
    stem = stem_mantissa[0]
    k_local, r_all, q_local = stem.shape[1:]
    k_all, l_half = branch.shape[1:]
    l_all = 2 * l_half
    r_local = closing.shape[1]
    expo = jnp.transpose(exponents[0], (0, 2, 1))
    bits = bitstrings.reshape(1, -1)
    dma = pltpu.SemaphoreType.DMA
    hbm = pl.BlockSpec(memory_space=pl.ANY)
    vmem = pl.BlockSpec(memory_space=pltpu.VMEM)
    done, product, received, matrix, amps = pl.pallas_call(
        contract_kernel,
        out_shape=(
            pltpu.VMEM((2 * l_all, r_local, 128), BF16),
            pltpu.VMEM((2 * l_all * r_local, 128), F32),
            pltpu.VMEM((4, 2, k_all // 4, q_local), BF16),
            pltpu.VMEM((2 * l_all, 2 * k_all), BF16),
            jax.ShapeDtypeStruct((2, bits.shape[1]), F32),
        ),
        in_specs=[hbm] * 5,
        out_specs=(vmem, vmem, vmem, vmem, hbm),
        scratch_shapes=[
            pltpu.VMEM((SLOTS, 2, k_local, 16, 128), BF16),
            pltpu.VMEM(expo.shape, jnp.int32),
            pltpu.VMEM((2, k_local, r_all), F32),
            pltpu.VMEM((2, 256, 128), F32),
            pltpu.VMEM((8, 2, r_local, 2, k_local, q_local), BF16),
            pltpu.VMEM((r_local - 1, 4, 2, k_all // 4, q_local), BF16),
            pltpu.VMEM((2 * l_all * r_local, 128), F32),
            pltpu.VMEM((2, k_all, l_half), BF16),
            pltpu.VMEM((2, k_all, l_half), BF16),
            pltpu.VMEM((2, k_local, l_half), BF16),
            pltpu.VMEM((2, 8) + closing.shape, BF16),
            pltpu.VMEM((2, 8, 2, 2, r_local, 128), F32),
            pltpu.VMEM(bits.shape, jnp.int32),
            pltpu.VMEM((16, 1, 128), F32),
            pltpu.VMEM((16, 1, 128), F32),
            pltpu.VMEM((2, 1, 128), F32),
            pltpu.VMEM((8, 1, 128), F32),
            pltpu.VMEM((16, 1, 128), F32),
            pltpu.VMEM((2, bits.shape[1]), F32),
            dma((SLOTS,)), dma((2,)), dma,
            dma((2 * ROUNDS,)), dma((4 * ROUNDS,)),
            dma, dma, dma, dma, dma, dma, dma, dma, dma, dma, dma, dma, dma, dma, dma, dma, dma, dma,
            pltpu.SemaphoreType.REGULAR, pltpu.SemaphoreType.REGULAR,
        ],
        compiler_params=pltpu.CompilerParams(
            collective_id=0, has_side_effects=True, vmem_limit_bytes=34 * 2**20
        ),
        cost_estimate=pl.CostEstimate(
            flops=2 * (2 * k_all) * (2 * l_all) * r_local * q_local, bytes_accessed=2 * stem.size, transcendentals=0
        ),
        name="exchange_and_contract",
    )(stem, expo, branch, closing, bits)

    rows = 128
    big = 512
    keep_vmem = [pltpu.with_memory_space_constraint(a, pltpu.VMEM) for a in (done, product, received, matrix)]
    new_block, amps = pl.pallas_call(
        write_kernel,
        out_shape=(
            jax.ShapeDtypeStruct((2, l_all, r_local, q_local), BF16),
            jax.ShapeDtypeStruct(amps.shape, F32),
        ),
        in_specs=[vmem, vmem, vmem, vmem, hbm],
        out_specs=(hbm, hbm),
        scratch_shapes=[
            pltpu.VMEM((2 * l_all // rows, rows, r_local, 128), BF16),
            pltpu.VMEM((big * r_local, 128), F32),
            dma((2,)),
            dma((2 * l_all // rows,)),
            dma,
        ],
        compiler_params=pltpu.CompilerParams(vmem_limit_bytes=34 * 2**20),
        name="finish_and_write",
    )(*keep_vmem, amps)
    return (new_block[None], amps)


def solution(mesh):
    return jax.shard_map(
        shards,
        mesh=mesh,
        in_specs=(
            P("cuts", None, "idx", None, "br"),
            P("cuts", "idx", None, "br"),
            P(None, None, "br"),
            P(None, "idx", "br"),
            P(),
        ),
        out_specs=(P("cuts", None, None, "idx", "br"), P()),
        check_vma=False,
    )
```

```python
import jax
import jax.numpy as jnp
from jax import lax
from jax.experimental import pallas as pl
from jax.experimental.pallas import tpu as pltpu
from jax.sharding import PartitionSpec as P

MESH = pl.DeviceIdType.MESH
F32 = jnp.float32
BF16 = jnp.bfloat16
ROUNDS = 8
DEPTH = 2
SLOTS = 4


def full_wait(ref, sem):
    pltpu.make_async_copy(ref, ref, sem).wait()


def contract_kernel(
    stem, expo, branch, closing, bits,
    done, product, latest, matrix, amps,
    inbuf, raw_exp, scale, tiles, sendbuf, recvbuf, first, own_half, other_half, other_rows,
    env_raw, env, bits_v, part, part_in, mid, mid_in, total_in, amps_v,
    in_sem, small_sem, half_sem, send_sem, recv_sem, near_send, half_send, half_recv, fwd_send, fwd_recv,
    rows_send, rows_recv, env_send, env_recv, share_send, share_recv, part_send, part_recv, mid_send, mid_recv, total_send, total_recv, amp_sem,
    ready, twin_ready,
):
    c = lax.axis_index("cuts")
    me = lax.axis_index("idx")
    b = lax.axis_index("br")
    core = me % 2
    x = (me // 2) % 4
    z = me // 8
    k_local, q_local = sendbuf.shape[4:]

    def steps(n, sender):
        dz = (1 - (n // 2) % 2) % 2
        dx = (2 + n % 2) * (1 - n // 4) + (1 - n % 2) * (n // 4)
        return dz, dx * (1 + 2 * sender) % 4

    def group(n):
        dz, dx = steps(n, core)
        return ((z + dz) % 2) * 4 + (x + dx) % 4

    def source_group(n, sender):
        dz, dx = steps(n, sender)
        return ((z + dz) % 2) * 4 + (x + 4 - dx) % 4

    def peer(step):
        return (c, (me + step) % 16, b)

    rank = b * 4 + c

    def outer(q):
        return (q % 4, me, q // 4)

    twin = (c, (me + 8) % 16, 1 - b)
    sibling = (c, me + 1 - 2 * core, b)

    def load(step):
        rows = pl.ds(pl.multiple_of(group(step % 8) * 16, 16), 16)
        columns = pl.ds(pl.multiple_of((step // 8) * 128, 128), 128)
        slot = step % SLOTS
        return pltpu.make_async_copy(stem.at[:, :, rows, columns], inbuf.at[slot], in_sem.at[slot])

    exp_copy = pltpu.make_async_copy(expo, raw_exp, small_sem.at[0])
    exp_copy.start()
    for step in range(SLOTS):
        load(step).start()

    barrier = pltpu.get_barrier_semaphore()
    for step in range(1, 16):
        pl.semaphore_signal(barrier, inc=1, device_id=peer(step), device_id_type=MESH)

    @pl.when(b == 0)
    def _():
        pl.semaphore_signal(barrier, inc=1, device_id=twin, device_id_type=MESH)

    for q in range(1, 8):
        @pl.when(q > rank)
        def _(q=q):
            pl.semaphore_signal(barrier, inc=1, device_id=outer(q), device_id_type=MESH)


    exp_copy.wait()
    for h in range(2):
        shifted = raw_exp[:, h, :] + 2
        low = (1 + shifted % 2).astype(F32)
        middle = (1 + 3 * ((shifted // 2) % 2)).astype(F32)
        high = (1 + 15 * ((shifted // 4) % 2)).astype(F32)
        scale[h] = 0.25 * low * middle * high

    def landing(n, dc, j, final):
        rows = pl.ds(pl.multiple_of((n % 4) * k_local, k_local), k_local)
        quarter = 2 * dc + n // 4
        return latest.at[quarter, :, rows, :] if final else recvbuf.at[j, quarter, :, rows, :]

    def message(n, dc, j, sem, final=False):
        cc = (core + dc) % 2
        return pltpu.make_async_remote_copy(
            src_ref=sendbuf.at[n, cc, j],
            dst_ref=landing(n, dc, j, final),
            send_sem=sem,
            recv_sem=recv_sem.at[4 * j + 2 * dc + n // 4],
            device_id=(c, group(n) * 2 + cc, b),
            device_id_type=MESH,
        )

    def keep(j, final=False):
        return pltpu.make_async_copy(sendbuf.at[7, core, j], landing(7, 0, j, final), recv_sem.at[4 * j + 1])

    def regroup(step):
        n = step % 8
        h = step // 8
        slot = step % SLOTS
        turn = (128 - group(n) * 16) % 128
        load(step).wait()

        def part_of_k(kb, carry):
            k0 = pl.multiple_of(kb * 16, 16)
            factors = pltpu.roll(scale[h, pl.ds(k0, 16), :], turn, 1)
            for p in range(2):
                tiles[p] = inbuf[slot, p, pl.ds(k0, 16)].astype(F32).reshape(256, 128)
            for r in range(16):
                factor = jnp.broadcast_to(factors[:, r:r + 1], (16, 128))
                spot = (r % 2) * 128
                for p in range(2):
                    rows = tiles[p, pl.ds(r, 16, stride=16), :] * factor
                    sendbuf[n, r // 8, 4 * h + r % 8 // 2, p, pl.ds(k0, 16), spot:spot + 128] = rows.astype(BF16)
            return carry

        lax.fori_loop(0, k_local // 16, part_of_k, 0)

    regroup(0)
    load(SLOTS).start()
    pl.semaphore_wait(barrier, 15 + rank + b)

    chip = me // 2

    def env_copy(step):
        return pltpu.make_async_remote_copy(
            src_ref=closing, dst_ref=env_raw.at[core, chip], send_sem=env_send, recv_sem=env_recv,
            device_id=peer(2 * step), device_id_type=MESH,
        )

    env_share = pltpu.make_async_remote_copy(
        src_ref=env_raw.at[core], dst_ref=env_raw.at[core], send_sem=share_send, recv_sem=share_recv,
        device_id=sibling, device_id_type=MESH,
    )

    half_rows = own_half.shape[1] // 2
    quarter = half_rows // 4

    def half_copy(t):
        rows = pl.ds(pl.multiple_of(core * half_rows + t * quarter, quarter), quarter)
        return pltpu.make_async_remote_copy(
            src_ref=branch.at[:, rows, :], dst_ref=other_half.at[:, rows, :],
            send_sem=half_send, recv_sem=half_recv, device_id=twin, device_id_type=MESH,
        )

    mine = pl.ds(pl.multiple_of(core * half_rows, half_rows), half_rows)
    theirs = pl.ds(pl.multiple_of((1 - core) * half_rows, half_rows), half_rows)
    forward = pltpu.make_async_remote_copy(
        src_ref=other_half.at[:, mine, :], dst_ref=other_half.at[:, mine, :],
        send_sem=fwd_send, recv_sem=fwd_recv, device_id=sibling, device_id_type=MESH,
    )
    twin_rows = pltpu.make_async_remote_copy(
        src_ref=branch.at[:, pl.ds(pl.multiple_of(((me + 8) % 16) * k_local, k_local), k_local), :],
        dst_ref=other_rows, send_sem=rows_send, recv_sem=rows_recv, device_id=twin, device_id_type=MESH,
    )


    @pl.when(b == 1)
    def _():
        pl.semaphore_signal(twin_ready, inc=1, device_id=twin, device_id_type=MESH)

    for q in range(7):
        @pl.when(q < rank)
        def _(q=q):
            pl.semaphore_signal(ready, inc=1, device_id=outer(q), device_id_type=MESH)

    message(0, 0, 0, send_sem.at[0]).start()
    message(0, 1, 0, send_sem.at[1]).start()

    def produce(n, carry):
        regroup(n)
        load(n + SLOTS).start()
        message(n, 0, 0, send_sem.at[0]).start()
        message(n, 1, 0, send_sem.at[1]).start()

        return carry

    lax.fori_loop(1, 7, produce, 0)
    regroup(7)
    load(7 + SLOTS).start()
    keep(0).start()
    message(7, 1, 0, near_send).start()
    bits_copy = pltpu.make_async_copy(bits, bits_v, small_sem.at[1])
    bits_copy.start()
    own_copy = pltpu.make_async_copy(branch, own_half, half_sem)
    own_copy.start()
    for step in range(1, 8):
        env_copy(step).start()
    pltpu.make_async_copy(closing, env_raw.at[core, chip], env_recv).start()

    def issue(h, final=False):
        j = h // 2
        dc = h % 2

        def start(n, carry):
            message(n, dc, j, send_sem.at[h], final).start()
            return carry

        lax.fori_loop(0, 7, start, 0)

        @pl.when(dc == 0)
        def _():
            keep(j, final).start()

        @pl.when(dc == 1)
        def _():
            message(7, 1, j, near_send, final).start()

    def drained(h):
        full_wait(sendbuf.at[0, 0, pl.ds(0, 7)], send_sem.at[h])

    k_all = own_half.shape[1]
    l_half = own_half.shape[2]

    def fill(half, where):
        def step(kb, carry):
            quarter = kb // 2
            place = (quarter % 2) * 4 + (kb % 2) * 2
            row = pl.multiple_of(where * l_half, l_half)
            column = pl.multiple_of(quarter * (k_all // 2) + (kb % 2) * 128, 128)

            def turned(p):
                pieces = []
                for extra in (0, 1):
                    sender = (core + quarter // 2) % 2
                    source = 2 * source_group(place + extra, sender) + sender
                    pieces.append(half[p, pl.ds(pl.multiple_of(source * k_local, k_local), k_local), :])
                return jnp.concatenate(pieces, axis=0).T

            real = turned(0)
            imag = turned(1)
            matrix[pl.ds(row, l_half), pl.ds(column, 128)] = real
            matrix[pl.ds(row, l_half), pl.ds(k_all // 4 + column, 128)] = -imag
            matrix[pl.ds(2 * l_half + row, l_half), pl.ds(column, 128)] = imag
            matrix[pl.ds(2 * l_half + row, l_half), pl.ds(k_all // 4 + column, 128)] = real
            return carry

        lax.fori_loop(0, k_all // 128, step, 0)

    issue(2)

    @pl.when(b == 0)
    def _():
        pl.semaphore_wait(twin_ready, 1)

    twin_rows.start()
    for t in range(4):
        half_copy(t).start()

    def second_half(step, carry):
        regroup(step)

        @pl.when(step + SLOTS < 16)
        def _():
            load(step + SLOTS).start()

        return carry

    lax.fori_loop(8, 16, second_half, 0)
    full_wait(env_raw.at[core], env_recv)
    env_share.start()
    own_copy.wait()

    for h in range(4 - DEPTH):
        drained(h)
    issue(3)
    full_wait(env_raw.at[1 - core], share_recv)
    for h in range(2):
        env[:, :, :, h] = env_raw[:, :, :, :, h * 128:(h + 1) * 128].astype(F32)

    def gather_env(n, sums):
        g = group(n)

        def row(t, sums):
            cc = t // 4
            pair = t % 4
            new = list(sums)
            for h in range(2):
                for p in range(2):
                    values = sendbuf[n, cc, 4 * h + pair, p].astype(F32)
                    for e in range(2):
                        for s in range(2):
                            weight = env[cc, g, e, h, pl.ds(2 * pair + s, 1), :]
                            new[2 * p + e] = new[2 * p + e] + values[:, s * 128:(s + 1) * 128] * weight
            return tuple(new)

        return lax.fori_loop(0, 8, row, sums)

    zero = jnp.zeros((k_local, 128), F32)
    sums = lax.fori_loop(0, 8, gather_env, (zero,) * 4)
    w = [jnp.sum(s, axis=1, keepdims=True) for s in sums]
    w_real = w[0] - w[3]
    w_imag = w[1] + w[2]

    k_mine = pl.ds(pl.multiple_of(me * k_local, k_local), k_local)
    blocks = l_half // 128
    full_wait(other_rows, rows_recv)
    for half, rows, where in ((own_half, k_mine, b), (other_rows, slice(None), 1 - b)):
        real = half[0, rows, :].astype(F32)
        imag = half[1, rows, :].astype(F32)
        closed_real = jnp.sum(real * w_real - imag * w_imag, axis=0, keepdims=True)
        closed_imag = jnp.sum(real * w_imag + imag * w_real, axis=0, keepdims=True)
        for t in range(blocks):
            part[where * blocks + t] = closed_real[:, t * 128:(t + 1) * 128]
            part[2 * blocks + where * blocks + t] = closed_imag[:, t * 128:(t + 1) * 128]

    def part_copy(step):
        to = (me + step) % 16
        return pltpu.make_async_remote_copy(
            src_ref=part.at[to], dst_ref=part_in.at[me], send_sem=part_send, recv_sem=part_recv,
            device_id=(c, to, b), device_id_type=MESH,
        )

    def mid_copy(q):
        return pltpu.make_async_remote_copy(
            src_ref=mid.at[0], dst_ref=mid_in.at[rank], send_sem=mid_send, recv_sem=mid_recv,
            device_id=outer(q), device_id_type=MESH,
        )

    def total_copy(step):
        return pltpu.make_async_remote_copy(
            src_ref=mid.at[1], dst_ref=total_in.at[me], send_sem=total_send, recv_sem=total_recv,
            device_id=peer(step), device_id_type=MESH,
        )

    for step in range(1, 16):
        part_copy(step).start()
    pltpu.make_async_copy(part.at[me], part_in.at[me], part_recv).start()

    drained(4 - DEPTH)
    issue(4)
    fill(own_half, b)

    drained(5 - DEPTH)
    issue(5)
    full_wait(part_in, part_recv)
    mid[0] = jnp.sum(part_in[...], axis=0)

    @pl.when(rank < 7)
    def _():
        pl.semaphore_wait(ready, 7 - rank)

    for q in range(8):
        @pl.when(q != rank)
        def _(q=q):
            mid_copy(q).start()

    pltpu.make_async_copy(mid.at[0], mid_in.at[rank], mid_recv).start()

    drained(6 - DEPTH)
    issue(6)
    full_wait(other_half.at[:, mine, :], half_recv)
    forward.start()
    full_wait(mid_in, mid_recv)
    mid[1] = jnp.sum(mid_in[...], axis=0)
    for step in range(1, 16):
        total_copy(step).start()
    pltpu.make_async_copy(mid.at[1], total_in.at[me], total_recv).start()

    drained(7 - DEPTH)
    issue(7)
    full_wait(other_half.at[:, theirs, :], fwd_recv)
    fill(other_half, 1 - b)

    drained(8 - DEPTH)
    issue(8)

    def choose():
        full_wait(total_in, total_recv)
        bits_copy.wait()
        chosen = bits_v[...]
        found = jnp.zeros((8, chosen.shape[1]), F32)
        for t in range(2 * blocks):
            rows = [total_in[t], total_in[2 * blocks + t], jnp.zeros((6, 128), F32)]
            spots = lax.broadcasted_iota(jnp.int32, (128, chosen.shape[1]), 0) + t * 128
            pick = jnp.where(spots == chosen, 1.0, 0.0).astype(F32)
            found = found + jnp.dot(
                jnp.concatenate(rows, axis=0), pick, precision=lax.Precision.HIGHEST, preferred_element_type=F32
            )
        amps_v[...] = found[:2]
        pltpu.make_async_copy(amps_v, amps, amp_sem).start()

    m_block = 512

    def tile_rows(m0, j, s):
        return pl.ds(m0 * ROUNDS + 2 * (j % 4) + s, m_block, stride=ROUNDS)

    def chunk(target):
        def run(j, carry):
            drained(j + 9 - DEPTH)

            @pl.when(j + 9 < 2 * ROUNDS - 2)
            def _():
                issue(j + 9)

            @pl.when(j + 9 >= 2 * ROUNDS - 2)
            def _():
                issue(j + 9, True)

            for quarter in range(4):
                full_wait(recvbuf.at[j, quarter], recv_sem.at[4 * j + quarter])

            def rows(m, carry):
                m0 = pl.multiple_of(m * m_block, m_block)
                right = recvbuf[j].reshape(2 * k_all, q_local)
                result = jnp.dot(matrix[pl.ds(m0, m_block), :], right, preferred_element_type=F32)
                for s in range(2):
                    target[tile_rows(m0, j, s), :] = result[:, s * 128:(s + 1) * 128]
                return carry

            lax.fori_loop(0, matrix.shape[0] // m_block, rows, 0)

            @pl.when(j == 2)
            def _():
                choose()

            return carry

        return run

    lax.fori_loop(0, ROUNDS // 2, chunk(first), 0)

    def settle(t, carry):
        t0 = pl.multiple_of(t * 128, 128)
        block = first[pl.ds(pl.multiple_of(t0 * ROUNDS, 128 * ROUNDS), 128 * ROUNDS), :]
        done[pl.ds(t0, 128)] = block.reshape(128, ROUNDS, 128).astype(BF16)
        return carry

    lax.fori_loop(0, matrix.shape[0] // 128, settle, 0)
    lax.fori_loop(ROUNDS // 2, ROUNDS - 1, chunk(product), 0)

    def early(low, high):
        columns = slice(low * (k_all // 2), high * (k_all // 2))

        def rows(m, carry):
            m0 = pl.multiple_of(m * m_block, m_block)
            right = latest[low:high].reshape((high - low) * (k_all // 2), q_local)
            result = jnp.dot(matrix[pl.ds(m0, m_block), columns], right, preferred_element_type=F32)
            for s in range(2):
                spots = tile_rows(m0, ROUNDS - 1, s)
                piece = result[:, s * 128:(s + 1) * 128]
                product[spots, :] = piece if low == 0 else product[spots, :] + piece
            return carry

        lax.fori_loop(0, matrix.shape[0] // m_block, rows, 0)

    last = 4 * (ROUNDS - 1)
    full_wait(latest.at[0], recv_sem.at[last])
    full_wait(latest.at[1], recv_sem.at[last + 1])
    early(0, 2)
    full_wait(latest.at[2], recv_sem.at[last + 2])
    full_wait(latest.at[3], recv_sem.at[last + 3])

    for h in range(2 * ROUNDS - DEPTH, 2 * ROUNDS):
        drained(h)
    full_wait(sendbuf.at[7, 0], near_send)
    full_wait(other_rows, rows_send)
    full_wait(env_raw.at[core], share_send)
    full_wait(other_half.at[:, mine, :], half_send)
    full_wait(other_half.at[:, mine, :], fwd_send)
    full_wait(env_raw.at[0, pl.ds(0, 7)], env_send)
    full_wait(part_in.at[pl.ds(0, 15)], part_send)
    full_wait(mid_in.at[pl.ds(0, 7)], mid_send)
    full_wait(total_in.at[pl.ds(0, 15)], total_send)
    full_wait(amps_v, amp_sem)


def write_kernel(
    done, product, latest, matrix, amps_in, out, amps, staging, spread, done_sem, out_sem, amp_sem
):
    amp_copy = pltpu.make_async_copy(amps_in, amps, amp_sem)
    amp_copy.start()
    blocks, rows = staging.shape[:2]
    l_all = out.shape[1]
    per_part = l_all // rows
    quarter = matrix.shape[1] // 4
    big = spread.shape[0] // ROUNDS
    whole = [
        pltpu.make_async_copy(done.at[pl.ds(p * l_all, l_all)], out.at[p, :, :, pl.ds(0, 128)], done_sem.at[p])
        for p in range(2)
    ]
    for copy in whole:
        copy.start()

    def copy(t):
        return pltpu.make_async_copy(
            staging.at[t],
            out.at[t // per_part, pl.ds((t % per_part) * rows, rows), :, pl.ds(128, 128)],
            out_sem.at[t],
        )

    def block(m, carry):
        m0 = pl.multiple_of(m * big, big)
        right = latest[2:].reshape(2 * quarter, latest.shape[3])
        result = jnp.dot(matrix[pl.ds(m0, big), 2 * quarter:], right, preferred_element_type=F32)
        for s in range(2):
            spread[pl.ds(ROUNDS - 2 + s, big, stride=ROUNDS), :] = result[:, s * 128:(s + 1) * 128]

        def piece(i, carry):
            t = m * (big // rows) + i
            spots = pl.ds(pl.multiple_of(t * rows * ROUNDS, rows * ROUNDS), rows * ROUNDS)
            local = pl.ds(pl.multiple_of(i * rows * ROUNDS, rows * ROUNDS), rows * ROUNDS)
            before = product[spots, :].reshape(rows, ROUNDS, 128)
            newest = spread[local, :].reshape(rows, ROUNDS, 128)
            spot = lax.broadcasted_iota(jnp.int32, (rows, ROUNDS, 128), 1)
            staging[t] = (before + jnp.where(spot >= ROUNDS - 2, newest, 0.0)).astype(BF16)
            copy(t).start()
            return carry

        lax.fori_loop(0, big // rows, piece, 0)
        return carry

    lax.fori_loop(0, matrix.shape[0] // big, block, 0)

    def finish(t, carry):
        copy(t).wait()
        return carry

    lax.fori_loop(0, blocks, finish, 0)
    for copy_of_part in whole:
        copy_of_part.wait()
    amp_copy.wait()


def shards(stem_mantissa, exponents, branch, closing, bitstrings):
    stem = stem_mantissa[0]
    k_local, r_all, q_local = stem.shape[1:]
    k_all, l_half = branch.shape[1:]
    l_all = 2 * l_half
    r_local = closing.shape[1]
    expo = jnp.transpose(exponents[0], (0, 2, 1))
    bits = bitstrings.reshape(1, -1)
    dma = pltpu.SemaphoreType.DMA
    hbm = pl.BlockSpec(memory_space=pl.ANY)
    vmem = pl.BlockSpec(memory_space=pltpu.VMEM)
    done, product, received, matrix, amps = pl.pallas_call(
        contract_kernel,
        out_shape=(
            pltpu.VMEM((2 * l_all, r_local, 128), BF16),
            pltpu.VMEM((2 * l_all * r_local, 128), F32),
            pltpu.VMEM((4, 2, k_all // 4, q_local), BF16),
            pltpu.VMEM((2 * l_all, 2 * k_all), BF16),
            jax.ShapeDtypeStruct((2, bits.shape[1]), F32),
        ),
        in_specs=[hbm] * 5,
        out_specs=(vmem, vmem, vmem, vmem, hbm),
        scratch_shapes=[
            pltpu.VMEM((SLOTS, 2, k_local, 16, 128), BF16),
            pltpu.VMEM(expo.shape, jnp.int32),
            pltpu.VMEM((2, k_local, r_all), F32),
            pltpu.VMEM((2, 256, 128), F32),
            pltpu.VMEM((8, 2, r_local, 2, k_local, q_local), BF16),
            pltpu.VMEM((r_local - 1, 4, 2, k_all // 4, q_local), BF16),
            pltpu.VMEM((2 * l_all * r_local, 128), F32),
            pltpu.VMEM((2, k_all, l_half), BF16),
            pltpu.VMEM((2, k_all, l_half), BF16),
            pltpu.VMEM((2, k_local, l_half), BF16),
            pltpu.VMEM((2, 8) + closing.shape, BF16),
            pltpu.VMEM((2, 8, 2, 2, r_local, 128), F32),
            pltpu.VMEM(bits.shape, jnp.int32),
            pltpu.VMEM((16, 1, 128), F32),
            pltpu.VMEM((16, 1, 128), F32),
            pltpu.VMEM((2, 1, 128), F32),
            pltpu.VMEM((8, 1, 128), F32),
            pltpu.VMEM((16, 1, 128), F32),
            pltpu.VMEM((2, bits.shape[1]), F32),
            dma((SLOTS,)), dma((2,)), dma,
            dma((2 * ROUNDS,)), dma((4 * ROUNDS,)),
            dma, dma, dma, dma, dma, dma, dma, dma, dma, dma, dma, dma, dma, dma, dma, dma, dma, dma,
            pltpu.SemaphoreType.REGULAR, pltpu.SemaphoreType.REGULAR,
        ],
        compiler_params=pltpu.CompilerParams(
            collective_id=0, has_side_effects=True, vmem_limit_bytes=34 * 2**20
        ),
        cost_estimate=pl.CostEstimate(
            flops=2 * (2 * k_all) * (2 * l_all) * r_local * q_local, bytes_accessed=2 * stem.size, transcendentals=0
        ),
        name="exchange_and_contract",
    )(stem, expo, branch, closing, bits)

    rows = 128
    big = 512
    keep_vmem = [pltpu.with_memory_space_constraint(a, pltpu.VMEM) for a in (done, product, received, matrix)]
    new_block, amps = pl.pallas_call(
        write_kernel,
        out_shape=(
            jax.ShapeDtypeStruct((2, l_all, r_local, q_local), BF16),
            jax.ShapeDtypeStruct(amps.shape, F32),
        ),
        in_specs=[vmem, vmem, vmem, vmem, hbm],
        out_specs=(hbm, hbm),
        scratch_shapes=[
            pltpu.VMEM((2 * l_all // rows, rows, r_local, 128), BF16),
            pltpu.VMEM((big * r_local, 128), F32),
            dma((2,)),
            dma((2 * l_all // rows,)),
            dma,
        ],
        compiler_params=pltpu.CompilerParams(vmem_limit_bytes=34 * 2**20),
        name="finish_and_write",
    )(*keep_vmem, amps)
    return (new_block[None], amps)


def solution(mesh):
    return jax.shard_map(
        shards,
        mesh=mesh,
        in_specs=(
            P("cuts", None, "idx", None, "br"),
            P("cuts", "idx", None, "br"),
            P(None, None, "br"),
            P(None, "idx", "br"),
            P(),
        ),
        out_specs=(P("cuts", None, None, "idx", "br"), P()),
        check_vma=False,
    )
```
